512 devices in a mesh: samp: 4 (over x_lo, core), var: 128 (over y, z, x_hi).
Axes of the slice: x: 4 (x_hi: 2, x_lo: 2; x = x_hi * 2 + x_lo), y: 8, z: 8, core: 2. Of those that a mesh axis runs over, the one named last changes fastest.
Arguments:
- genotypes: int32 [256, 16384], P('samp', 'var'), may hold values from 0 to 2
- covariates: float32 [256, 40], P('samp'), may hold values from -6 to 6
- traits: float32 [256, 8], P('samp'), may hold values from -6 to 6
- trait_weights: float32 [8], replicated, may hold values from 0.25 to 2
Outputs:
- block_scores: float32 [16384, 128], P('var')
The draws below stay inside these ranges and needn't reach their ends.
All inputs are finite; a program needn't handle non-finite values.
Results may differ from the reference program's by a relative error of at most 0.0003.
Values sent between devices are 32-bit elements; how exact they have to be, the bound alone decides.
A program may use at most 64 MiB of HBM per device.

```python
import math
import jax
import jax.numpy as jnp
from jax import lax

NC = 40
NT = 8
VB = 128
SAMPLES = 256
VARIANTS = 16384
HALF = 64
N_VAR = 128


def with_ends(values, rng, least, largest):
    longest = values.shape.index(max(values.shape))
    spots = []
    for shift in (0, 1):
        where = [jax.random.randint(jax.random.fold_in(rng, axis), (), 0, length) for axis, length in enumerate(values.shape)]
        where[longest] = (where[longest] + shift) % values.shape[longest]
        spots.append(tuple(where))
    return values.at[spots[0]].set(least).at[spots[1]].set(largest)


def steps_of(stream_key, shape, pieces, least, largest):
    gain = 1.0
    for axis_at, shards_of in pieces:
        draws = jax.random.uniform(jax.random.fold_in(jax.random.fold_in(stream_key, 6), axis_at), (shards_of,), jnp.float32, least / len(pieces), largest / len(pieces))
        gain = gain * jnp.repeat(jnp.exp(draws), shape[axis_at] // shards_of).reshape((-1,) + (1,) * (len(shape) - 1 - axis_at))
    return gain


def normal_values(stream_key, shape, width, limit, cuts=(), kind=jnp.bfloat16):
    entries = jax.random.normal(stream_key, shape, jnp.float32) * width
    if len(cuts) > 0:
        entries = steps_of(stream_key, shape, cuts, -0.22, 0.18) * entries
    return jnp.clip(entries, min=-limit, max=limit).astype(kind)


def setup_inputs(seed: int = 0) -> dict:
    key_of = jax.random.split(jax.random.key(seed), 5)
    genotypes = with_ends(jax.random.randint(key_of[0], (SAMPLES, VARIANTS), 0, 3), jax.random.fold_in(key_of[0], 1), 0, 2).astype(jnp.int32)
    covariates = normal_values(key_of[1], (SAMPLES, NC), 1.0, 6.0, ((0, 4),), jnp.float32)
    traits = normal_values(key_of[2], (SAMPLES, NT), 1.0, 6.0, ((0, 4),), jnp.float32)
    trait_weights = jnp.clip(jnp.exp(jax.random.uniform(key_of[3], (NT,), jnp.float32, math.log(0.25), math.log(2.0))), 0.25, 2.0)
    return dict(genotypes=genotypes, covariates=covariates, traits=traits, trait_weights=trait_weights)


def reference(genotypes, covariates, traits, trait_weights):
    highest = lax.Precision.HIGHEST
    centred = genotypes.astype(jnp.float32) - 1.0
    cov_count = covariates.shape[1]
    cross = jnp.dot(covariates.T, covariates, precision=highest)
    cross = cross + SAMPLES / 10.0 * jnp.eye(cov_count, dtype=jnp.float32)
    factor = jnp.linalg.cholesky(cross)
    coef_g = jax.scipy.linalg.cho_solve((factor, True), jnp.dot(covariates.T, centred, precision=highest))
    coef_y = jax.scipy.linalg.cho_solve((factor, True), jnp.dot(covariates.T, traits, precision=highest))
    resid = centred - jnp.dot(covariates, coef_g, precision=highest)
    yscaled = (traits - jnp.dot(covariates, coef_y, precision=highest)) * (1.0 / math.sqrt(SAMPLES))
    blocks = resid.reshape(SAMPLES, N_VAR, VB)
    offsets = jnp.arange(HALF + 1, dtype=jnp.int32)
    col_keep = ((offsets > 0) & (offsets < HALF)).astype(jnp.float32)
    off_diagonal = 1.0 - jnp.eye(VB, dtype=jnp.float32)

    def visit(scores, source):
        own_block = lax.dynamic_index_in_dim(blocks, source, 1, keepdims=False)
        weighted = own_block[:, None, :] * yscaled[:, :, None]
        targets = (source - offsets) % N_VAR
        panels = jnp.take(blocks, targets, axis=1)
        statistic = jnp.einsum('sti,skj->tikj', weighted, panels, precision=highest)
        pair_stat = jnp.einsum('t,tikj->ikj', trait_weights, statistic * statistic, precision=highest)
        pair_stat = pair_stat.at[:, 0, :].multiply(off_diagonal)
        row_sums = lax.optimization_barrier(jnp.sum(pair_stat, axis=2))
        col_sums = lax.optimization_barrier(jnp.sum(pair_stat, axis=0)) * col_keep[:, None]
        scores = scores.at[source, :, targets].add(row_sums.T)
        scores = scores.at[targets, :, source].add(col_sums)
        return (scores, None)
    scores, _ = lax.scan(visit, jnp.zeros((N_VAR, VB, N_VAR), jnp.float32), jnp.arange(N_VAR, dtype=jnp.int32))
    return scores.reshape(N_VAR * VB, N_VAR) / VB
```

```python
import functools
import math

import jax
import jax.numpy as jnp
from jax import lax
from jax.experimental import pallas as pl
from jax.experimental.pallas import tpu as pltpu
from jax.sharding import PartitionSpec as P

MESH = pl.DeviceIdType.MESH
HIGHEST = lax.Precision.HIGHEST
SIDE = 4
SLOTS = 2 * SIDE + 1
EXTRA = 2 * SIDE


def dot(a, b, contract=((1,), (0,)), precision=None):
    return lax.dot_general(
        a, b, (contract, ((), ())), precision=precision, preferred_element_type=jnp.float32
    )


def split(value):
    high = value.astype(jnp.bfloat16)
    return high, (value - high.astype(jnp.float32)).astype(jnp.bfloat16)


def inverse(matrix, size):
    rows = lax.broadcasted_iota(jnp.int32, (size, size), 0)
    cols = lax.broadcasted_iota(jnp.int32, (size, size), 1)
    for k in range(size):
        row = matrix[k : k + 1, :]
        column = matrix[:, k : k + 1]
        scale = 1.0 / matrix[k : k + 1, k : k + 1]
        left = jnp.where(rows == k, -1.0, column)
        right = jnp.where(cols == k, -1.0, row) * scale
        matrix = jnp.where((rows == k) | (cols == k), 0.0, matrix) - left * right
    return -matrix


def kernel(
    geno, cov, trait, tw_row, tw_col, out,
    gbuf, covb, traitb, pcat, qmat, ysc, hcat, rcat, rfull, tiles, landed, sum_a, sum_b, extra_row,
    send_sem, recv_sem, small_send, small_recv, own_sem, out_send, out_recv,
):
    section = lax.axis_index("samp")
    block = lax.axis_index("var")
    l, k = section // 2, section % 2
    h, z, y = block % 2, (block // 2) % 8, block // 16
    same = (h == l).astype(jnp.int32)
    shift = (1 - l) * (k * (1 - h) + h) + l * (h * k)

    def index(yy, zz, hh):
        return ((yy + 16) % 8 * 8 + (zz + 16) % 8) * 2 + hh

    def side_block(slot):
        if slot < SIDE:
            return index(y, z + shift + slot, h)
        if slot < EXTRA:
            return index(y + 4 * k + slot - SIDE, z, l)
        return index(y, z + 4 * (1 - k), h)

    def is_me(samp, var):
        return (samp == section) & (var == block)

    users = []
    for i in range(2):
        for kk in range(2):
            first = kk * (1 - h) + h if i == 0 else h * kk
            for a in range(SIDE):
                users.append((a, 2 * i + kk, index(y, z - first - a, h)))
    for j in range(2):
        for kk in range(2):
            for b in range(SIDE):
                users.append((SIDE + b, 2 * h + kk, index(y - 4 * kk - b, z, j)))
    users.append((EXTRA, 2 * h, index(y, z + 4, h)))
    users.append((EXTRA, 2 * h + 1, block))

    own_cov = pltpu.make_async_copy(cov, covb.at[section], own_sem.at[0])
    own_trait = pltpu.make_async_copy(trait, traitb.at[section], own_sem.at[1])
    own_cov.start()
    own_trait.start()

    barrier = pltpu.get_barrier_semaphore()
    for step in range(1, 4):
        pl.semaphore_signal(barrier, inc=1, device_id=((section + step) % 4, block), device_id_type=MESH)
    for slot in range(SLOTS):
        owner = side_block(slot)
        for q in range(4):
            wanted = jnp.logical_not(is_me(q, owner))
            if slot == EXTRA:
                wanted = wanted & (same == 1)

            @pl.when(wanted)
            def _():
                pl.semaphore_signal(barrier, inc=1, device_id=(q, owner), device_id_type=MESH)

    selves = same + (shift == 0).astype(jnp.int32)
    pl.semaphore_wait(barrier, len(users) + 3 - selves)

    small = []
    for step in range(1, 4):
        peer = ((section + step) % 4, block)
        for n, (src, dst) in enumerate(((cov, covb), (trait, traitb))):
            small.append(
                pltpu.make_async_remote_copy(
                    src_ref=src, dst_ref=dst.at[section], send_sem=small_send.at[n, step - 1],
                    recv_sem=small_recv.at[n, 3 - step], device_id=peer, device_id_type=MESH,
                )
            )
    for copy in small:
        copy.start()

    remotes = []
    for n, (slot, samp, var) in enumerate(users):
        mine = is_me(samp, var)
        remote = pltpu.make_async_remote_copy(
            src_ref=geno, dst_ref=gbuf.at[slot, section], send_sem=send_sem.at[n],
            recv_sem=recv_sem.at[slot], device_id=(samp, var), device_id_type=MESH,
        )
        remotes.append((mine, remote))
        pl.when(jnp.logical_not(mine))(remote.start)
        pl.when(mine)(pltpu.make_async_copy(geno, gbuf.at[slot, section], recv_sem.at[slot]).start)

    own_cov.wait()
    own_trait.wait()
    for copy in small:
        copy.wait()

    count, width = covb.shape[0] * covb.shape[1], covb.shape[2]
    covs = covb[...].reshape(count, width)
    traits = traitb[...].reshape(count, traitb.shape[2])
    eye = (
        lax.broadcasted_iota(jnp.int32, (width, width), 0)
        == lax.broadcasted_iota(jnp.int32, (width, width), 1)
    ).astype(jnp.float32)
    cross = dot(covs, covs, ((0,), (0,)), HIGHEST) + count / 10.0 * eye
    solved = dot(covs, inverse(cross, width), precision=HIGHEST)
    hat = dot(solved, covs, ((1,), (1,)), HIGHEST)
    diagonal = lax.broadcasted_iota(jnp.int32, (count, count), 0) == lax.broadcasted_iota(
        jnp.int32, (count, count), 1
    )
    project = jnp.where(diagonal, 1.0, 0.0) - hat
    high, low = split(project)
    pcat[:, :count] = high
    pcat[:, count:] = low
    scaled = dot(project, traits, precision=HIGHEST) * (1.0 / math.sqrt(count))
    ysc[...] = scaled
    qmat[...] = dot(scaled * tw_row[...], scaled, ((1,), (1,)), HIGHEST)

    def arrive(slot):
        pltpu.make_async_copy(gbuf.at[slot], gbuf.at[slot], recv_sem.at[slot]).wait()
        centred = (gbuf[slot].astype(jnp.float32) - 1.0).astype(jnp.bfloat16)
        centred = centred.reshape(count, centred.shape[-1])
        return dot(pcat[...], jnp.concatenate([centred, centred], axis=0))

    def make_h(slot, high, low):
        wide = jnp.concatenate([high, low], axis=1)
        twice = jnp.concatenate([high, high], axis=1)
        gram = dot(wide, twice, ((1,), (1,))) + dot(high, low, ((1,), (1,)))
        h_high, h_low = split(gram * qmat[...])
        rows = pl.ds(pl.multiple_of(slot * count, count), count)
        hcat[rows, :count] = h_high
        hcat[rows, count : 2 * count] = h_high
        hcat[rows, 2 * count :] = h_low

    def prepare(slot, carry):
        resid = arrive(slot)
        high, low = split(resid)
        side, at = slot // SIDE, pl.ds(pl.multiple_of(slot % SIDE * 128, 128), 128)
        rfull[side, :, at] = resid
        rcat[side, :count, at] = high
        rcat[side, count : 2 * count, at] = low
        rcat[side, 2 * count :, at] = high
        make_h(slot, high, low)
        return carry

    lax.fori_loop(0, EXTRA, prepare, 0)

    def score(step, carry):
        side, part = step // 2, step % 2
        at = pl.ds(pl.multiple_of(part * 256, 256), 256)
        rows = pl.ds(pl.multiple_of((1 - side) * SIDE * count, SIDE * count), SIDE * count)
        product = dot(hcat[rows, :], rcat[side, :, at])
        weighted = product.reshape(SIDE, count, 256) * rfull[side, :, at][None]
        sums = jnp.sum(weighted, axis=1)
        sums = jnp.concatenate([sums, jnp.zeros_like(sums)], axis=0)
        sums = pltpu.roll(sums, jnp.where(side == 0, 4 * k, shift), 0)
        first = side * SIDE + part * 2
        tiles[first] = sums[:, :128]
        tiles[first + 1] = sums[:, 128:]
        return carry

    lax.fori_loop(0, 4, score, 0)

    row_ids = lax.broadcasted_iota(jnp.int32, (8, 128), 0)

    @pl.when(same == 1)
    def _():
        high, low = split(arrive(EXTRA))
        make_h(EXTRA, high, low)
        product = dot(hcat[EXTRA * count :, :], rcat[1, :, :128])
        extra = jnp.sum(product * rfull[1, :, :128], axis=0, keepdims=True)
        tile = jnp.where(row_ids == 4 * k, 0.0, tiles[SIDE])
        tiles[SIDE] = jnp.where(row_ids == 4 * (1 - k), extra, tile)

    @pl.when((same == 1) & (k == 0))
    def _():
        resid = rfull[0, :, :128]
        own = dot(ysc[...], resid * resid, ((0,), (0,)), HIGHEST)
        own = jnp.sum(own * own * tw_col[...], axis=0, keepdims=True)
        tiles[0] = tiles[0] - jnp.where(row_ids == 0, own, 0.0)

    returns = []
    for slot in range(EXTRA):
        owner = side_block(slot)
        at = l * 8 + k * 4 + slot if slot < SIDE else 16 + h * 8 + k * 4 + slot - SIDE
        for q in range(4):
            mine = is_me(q, owner)
            remote = pltpu.make_async_remote_copy(
                src_ref=tiles.at[slot], dst_ref=landed.at[at], send_sem=out_send.at[slot * 4 + q],
                recv_sem=out_recv, device_id=(q, owner), device_id_type=MESH,
            )
            returns.append((mine, remote))
            pl.when(jnp.logical_not(mine))(remote.start)
            pl.when(mine)(pltpu.make_async_copy(tiles.at[slot], landed.at[at], out_recv).start)

    sum_a[...] = jnp.zeros_like(sum_a)
    for mine, remote in remotes + returns:
        pl.when(jnp.logical_not(mine))(remote.wait_send)
    pltpu.make_async_copy(landed, landed, out_recv).wait()

    for i in range(2):
        for kk in range(2):
            first = kk * (1 - h) + h if i == 0 else h * kk
            for n in range(SIDE):
                at = i * 8 + kk * 4 + n
                there = pl.ds((z + 8 - first - n) % 8 * 2 + i, 8, stride=16)
                sum_a[there, :] = sum_a[there, :] + pltpu.roll(landed[at], y, 0)
                there = pl.ds((y + 8 - 4 * kk - n) % 8 * 16 + i, 8, stride=2)
                sum_b[there, :] = pltpu.roll(landed[16 + at], z, 0)
    out[...] = (sum_a[...] + sum_b[...]).T * (1.0 / out.shape[0])


def body(genotypes, covariates, traits, trait_weights):
    part, width = genotypes.shape
    count = 4 * part
    cov_count, trait_count = covariates.shape[1], traits.shape[1]
    f32, bf16 = jnp.float32, jnp.bfloat16
    anywhere = pl.BlockSpec(memory_space=pl.ANY)
    vmem = pl.BlockSpec(memory_space=pltpu.VMEM)
    dma = pltpu.SemaphoreType.DMA
    return pl.pallas_call(
        kernel,
        name="epistasis",
        out_shape=jax.ShapeDtypeStruct((width, 128), f32),
        in_specs=[anywhere, anywhere, anywhere, vmem, vmem],
        out_specs=vmem,
        scratch_shapes=[
            pltpu.VMEM((SLOTS, 4, part, width), jnp.int32),
            pltpu.VMEM((4, part, cov_count), f32),
            pltpu.VMEM((4, part, trait_count), f32),
            pltpu.VMEM((count, 2 * count), bf16),
            pltpu.VMEM((count, count), f32),
            pltpu.VMEM((count, trait_count), f32),
            pltpu.VMEM((SLOTS * count, 3 * count), bf16),
            pltpu.VMEM((2, 3 * count, SIDE * width), bf16),
            pltpu.VMEM((2, count, SIDE * width), f32),
            pltpu.VMEM((EXTRA, 8, width), f32),
            pltpu.VMEM((32, 8, width), f32),
            pltpu.VMEM((128, width), f32),
            pltpu.VMEM((128, width), f32),
            pltpu.VMEM((8, width), f32),
            dma((34,)), dma((SLOTS,)), dma((2, 3)), dma((2, 3)), dma((2,)), dma((32,)), dma,
        ],
        compiler_params=pltpu.CompilerParams(
            collective_id=0, has_side_effects=True, vmem_limit_bytes=48 << 20
        ),
    )(genotypes, covariates, traits, trait_weights[None, :], trait_weights[:, None])


def solution(mesh):
    placed = (P("samp", "var"), P("samp", None), P("samp", None), P())
    return jax.shard_map(
        body, mesh=mesh, in_specs=placed, out_specs=P("var", None), check_vma=False
    )
```

```python
import math

import jax
import jax.numpy as jnp
from jax import lax
from jax.experimental import pallas as pl
from jax.experimental.pallas import tpu as pltpu
from jax.sharding import PartitionSpec as P

MESH = pl.DeviceIdType.MESH
HIGHEST = lax.Precision.HIGHEST
SIDE = 4
ALONG_Z = (0, 1, 2, -3, 4)
A_SLOTS = len(ALONG_Z)


def dot(a, b, contract=((1,), (0,)), precision=None):
    return lax.dot_general(
        a, b, (contract, ((), ())), precision=precision, preferred_element_type=jnp.float32
    )


def split(value):
    high = value.astype(jnp.bfloat16)
    return high, (value - high.astype(jnp.float32)).astype(jnp.bfloat16)


def sweep(matrix, begin, end):
    size = matrix.shape[0]
    rows = lax.broadcasted_iota(jnp.int32, (size, size), 0)
    cols = lax.broadcasted_iota(jnp.int32, (size, size), 1)
    for k in range(begin, end, 2):
        row_1, row_2 = matrix[k : k + 1, :], matrix[k + 1 : k + 2, :]
        col_1, col_2 = matrix[:, k : k + 1], matrix[:, k + 1 : k + 2]
        p, q, r = row_1[:, k : k + 1], row_1[:, k + 1 : k + 2], row_2[:, k + 1 : k + 2]
        scale = 1.0 / (p * r - q * q)
        row_1 = jnp.where(cols == k, -1.0, jnp.where(cols == k + 1, 0.0, row_1))
        row_2 = jnp.where(cols == k + 1, -1.0, jnp.where(cols == k, 0.0, row_2))
        col_1 = jnp.where(rows == k, -1.0, jnp.where(rows == k + 1, 0.0, col_1))
        col_2 = jnp.where(rows == k + 1, -1.0, jnp.where(rows == k, 0.0, col_2))
        kept = (rows == k) | (rows == k + 1) | (cols == k) | (cols == k + 1)
        matrix = (
            jnp.where(kept, 0.0, matrix)
            - col_1 * ((r * row_1 - q * row_2) * scale)
            - col_2 * ((p * row_2 - q * row_1) * scale)
        )
    return matrix


def kernel(
    geno, cov, trait, weights, out,
    line, abuf, bbuf, covb, traitb, tw, pcat, qmat, ysc, hcat, rcat_a, rcat_b, rfull_a, rfull_b,
    tiles, landed, sum_a, sum_b,
    z_send, z_recv, y_send, y_recv, bx_send, bx_recv, ax_send, ax_recv, core_send, core_recv,
    small_send, small_recv, own_sem, out_send, out_recv,
):
    section = lax.axis_index("samp")
    block = lax.axis_index("var")
    l, k = section // 2, section % 2
    h, z, y = block % 2, (block // 2) % 8, block // 16
    same = (h == l).astype(jnp.int32)
    shift = same * k + (1 - same) * h

    def index(yy, zz, hh):
        return ((yy + 16) % 8 * 8 + (zz + 16) % 8) * 2 + hh

    def samp(ll, kk):
        return 2 * ll + kk

    def is_me(target):
        return (target[0] == section) & (target[1] == block)

    def unless_me(target, action):
        pl.when(jnp.logical_not(is_me(target)))(action)

    def send(src, dst, send_sem, recv_sem, target):
        return pltpu.make_async_remote_copy(
            src_ref=src, dst_ref=dst, send_sem=send_sem, recv_sem=recv_sem,
            device_id=target, device_id_type=MESH,
        )

    def send_or_copy(src, dst, send_sem, recv_sem, target):
        mine = is_me(target)
        remote = send(src, dst, send_sem, recv_sem, target)
        pl.when(jnp.logical_not(mine))(remote.start)
        pl.when(mine)(pltpu.make_async_copy(src, dst, recv_sem).start)
        return lambda: unless_me(target, remote.wait_send)

    def landing(ref, sem):
        pltpu.make_async_copy(ref, ref, sem).wait()

    own = [
        pltpu.make_async_copy(cov, covb.at[2 * k + l], own_sem.at[0]),
        pltpu.make_async_copy(trait, traitb.at[2 * k + l], own_sem.at[1]),
        pltpu.make_async_copy(weights, tw, own_sem.at[2]),
    ]
    for copy in own:
        copy.start()

    peers = [((section + step) % 4, block) for step in range(1, 4)]
    z_targets = [(section, index(y, z - d, h)) for d in ALONG_Z[1:]]
    z_sources = [(section, index(y, z + d, h)) for d in ALONG_Z[1:]]
    y_targets = [(samp(l, e // SIDE), index(y - e, z, h)) for e in range(8)]
    y_sources = [
        (samp(l, kk), index(y + 4 * k + b, z, h)) for b in range(SIDE) for kk in range(2)
    ]
    beside = (samp(1 - l, k), block)
    sibling = (samp(l, 1 - k), block)
    ax_targets = [(samp(h, k), index(y, z, hh)) for hh in range(2)]
    ax_sources = [(samp(ll, k), index(y, z, l)) for ll in range(2)]

    barrier = pltpu.get_barrier_semaphore()
    for source in peers + z_sources + y_sources + [beside, sibling] + ax_sources:
        unless_me(
            source,
            lambda source=source: pl.semaphore_signal(
                barrier, inc=1, device_id=source, device_id_type=MESH
            ),
        )
    pl.semaphore_wait(barrier, 19 - (1 - k) - same)

    sent = []
    small = []
    for n, peer in enumerate(peers):
        for m, (src, dst) in enumerate(((cov, covb), (trait, traitb))):
            copy = send(src, dst.at[2 * k + l], small_send.at[m, n], small_recv.at[m, 2 - n], peer)
            copy.start()
            small.append(copy)
    for n in reversed(range(4)):
        copy = send(geno, line.at[n], z_send.at[n], z_recv.at[n], z_targets[n])
        copy.start()
        sent.append(copy.wait_send)
    for e in (4, 3, 5, 2, 6, 1, 7, 0):
        dst = bbuf.at[e % SIDE, k, l]
        sent.append(send_or_copy(geno, dst, y_send.at[e], y_recv.at[e % SIDE], y_targets[e]))

    def pass_a(slot):
        src = geno if slot == 0 else line.at[slot - 1]
        if slot > 0:
            landing(src, z_recv.at[slot - 1])
        for n, target in enumerate(ax_targets):
            dst = abuf.at[slot, k, l]
            sent.append(send_or_copy(src, dst, ax_send.at[slot, n], ax_recv.at[slot], target))

    def pass_b(step):
        slot = step + k * (SIDE - 1 - 2 * step)
        half = bbuf.at[slot, :, l]
        landing(half, y_recv.at[slot])
        copy = send(half, half, bx_send.at[step], bx_recv.at[slot], beside)
        copy.start()
        sent.append(copy.wait_send)

    def pass_core(slot):
        part = abuf.at[slot, k]
        landing(part, ax_recv.at[slot])
        copy = send(part, part, core_send.at[slot], core_recv.at[slot], sibling)
        copy.start()
        sent.append(copy.wait_send)

    pass_a(0)
    for copy in own + small:
        copy.wait()
    cov_t = jnp.concatenate([covb[n] for n in range(4)], axis=1)
    trait_t = jnp.concatenate([traitb[n] for n in range(4)], axis=1)
    width, count = cov_t.shape
    eye = (
        lax.broadcasted_iota(jnp.int32, (width, width), 0)
        == lax.broadcasted_iota(jnp.int32, (width, width), 1)
    ).astype(jnp.float32)
    swept = dot(cov_t, cov_t, ((1,), (1,)), HIGHEST) + count / 10.0 * eye
    pass_a(1)
    pass_b(0)
    swept = sweep(swept, 0, width // 4)
    pass_b(1)
    swept = sweep(swept, width // 4, width // 2)
    pass_a(2)
    pass_core(0)
    swept = sweep(swept, width // 2, width * 3 // 4)
    pass_a(3)
    pass_b(2)
    swept = sweep(swept, width * 3 // 4, width)
    pass_core(1)
    solved = dot(-swept, cov_t, precision=HIGHEST)
    hat = dot(cov_t, solved, ((0,), (0,)), HIGHEST)
    diagonal = lax.broadcasted_iota(jnp.int32, (count, count), 0) == lax.broadcasted_iota(
        jnp.int32, (count, count), 1
    )
    project = jnp.where(diagonal, 1.0, 0.0) - hat
    high, low = split(project)
    pcat[:, :count] = high
    pcat[:, count:] = low
    pass_b(3)
    pass_a(4)
    pass_core(2)
    scaled = dot(trait_t, project, precision=HIGHEST) * (1.0 / math.sqrt(count))
    ysc[...] = scaled
    traits_id = lax.broadcasted_iota(jnp.int32, (scaled.shape[0], 1), 0)
    tw_col = sum(jnp.where(traits_id == t, tw[t], 0.0) for t in range(scaled.shape[0]))
    qmat[...] = dot(scaled * tw_col, scaled, ((0,), (0,)), HIGHEST)
    pass_core(3)
    pass_core(4)

    def prepare(genotypes, at, rcat, rfull, hrow):
        centred = (genotypes.astype(jnp.float32) - 1.0).astype(jnp.bfloat16).reshape(count, 128)
        resid = dot(pcat[...], jnp.concatenate([centred, centred], axis=0))
        high, low = split(resid)
        at = pl.ds(pl.multiple_of(at * 128, 128), 128)
        rfull[:, at] = resid
        rcat[:count, at] = high
        rcat[count : 2 * count, at] = low
        rcat[2 * count :, at] = high
        wide = jnp.concatenate([high, low], axis=1)
        twice = jnp.concatenate([high, high], axis=1)
        gram = dot(wide, twice, ((1,), (1,))) + dot(high, low, ((1,), (1,)))
        h_high, h_low = split(gram * qmat[...])
        rows = pl.ds(pl.multiple_of(hrow * count, count), count)
        hcat[rows, :count] = h_high
        hcat[rows, count : 2 * count] = h_high
        hcat[rows, 2 * count :] = h_low

    def prepare_b(step, carry):
        slot = step + k * (SIDE - 1 - 2 * step)
        landing(bbuf.at[slot, :, 1 - l], bx_recv.at[slot])
        prepare(bbuf[slot], slot, rcat_b, rfull_b, A_SLOTS + slot)
        return carry

    def prepare_a(slot, carry):
        landing(abuf.at[slot, 1 - k], core_recv.at[slot])
        prepare(abuf[slot], slot, rcat_a, rfull_a, slot)
        return carry

    lax.fori_loop(0, SIDE, prepare_b, 0)
    lax.fori_loop(0, A_SLOTS, prepare_a, 0)

    def pairs(hrow, rcat, rfull, at):
        at = pl.ds(pl.multiple_of(at * 128, 128), 256)
        rows = pl.ds(pl.multiple_of(hrow * count, count), SIDE * count)
        product = dot(hcat[rows, :], rcat[:, at])
        weighted = product.reshape(SIDE, count, 256) * rfull[:, at][None]
        sums = jnp.sum(weighted, axis=1)
        return jnp.concatenate([sums, jnp.zeros_like(sums)], axis=0)

    def score_a(part, carry):
        sums = pairs(A_SLOTS, rcat_a, rfull_a, shift + 2 * part)
        sums = pltpu.roll(sums, 4 * k, 0)
        tiles[2 * part] = sums[:, :128]
        tiles[2 * part + 1] = sums[:, 128:]
        return carry

    def by_offset(sums):
        sums = pltpu.roll(sums, shift, 0)
        picked = [sums[a : a + 1] for a in (0, 1, 2, 5, 4, 3, 6, 7)]
        return jnp.concatenate(picked, axis=0)

    def score_b(part, carry):
        sums = by_offset(pairs(shift, rcat_b, rfull_b, 2 * part))
        tiles[SIDE + 2 * part] = sums[:, :128]
        tiles[SIDE + 2 * part + 1] = sums[:, 128:]
        return carry

    lax.fori_loop(0, 2, score_b, 0)
    lax.fori_loop(0, 2, score_a, 0)

    row_ids = lax.broadcasted_iota(jnp.int32, (8, 128), 0)

    @pl.when(same == 1)
    def _():
        rows = pl.ds(pl.multiple_of((1 - k) * 4 * count, count), count)
        product = dot(hcat[rows, :], rcat_b[:, :128])
        extra = jnp.sum(product * rfull_b[:, :128], axis=0, keepdims=True)
        tile = jnp.where(row_ids == 4 * k, 0.0, tiles[SIDE])
        tiles[SIDE] = jnp.where(row_ids == 4 * (1 - k), extra, tile)

    @pl.when((same == 1) & (k == 0))
    def _():
        resid = rfull_a[:, :128]
        diag = dot(ysc[...], resid * resid, precision=HIGHEST)
        diag = jnp.sum(diag * diag * tw_col, axis=0, keepdims=True)
        tiles[0] = tiles[0] - jnp.where(row_ids == 0, diag, 0.0)

    for slot in range(2 * SIDE):
        if slot < SIDE:
            offset = jnp.where(shift == 0, ALONG_Z[slot], ALONG_Z[slot + 1])
            owner, at = index(y, z + offset, l), h * 8 + k * 4 + slot
        else:
            owner, at = index(y + 4 * k + slot - SIDE, z, h), 16 + l * 8 + k * 4 + slot - SIDE
        for q in range(4):
            sent.append(
                send_or_copy(
                    tiles.at[slot], landed.at[at], out_send.at[slot * 4 + q], out_recv, (q, owner)
                )
            )

    sum_a[...] = jnp.zeros_like(sum_a)
    for wait in sent:
        wait()
    landing(landed, out_recv)

    for i in range(2):
        mixed = jnp.not_equal(h, i).astype(jnp.int32)
        for kk in range(2):
            first = mixed * (1 - h) + (1 - mixed) * kk
            for n in range(SIDE):
                at = i * 8 + kk * 4 + n
                offset = jnp.where(first == 0, ALONG_Z[n], ALONG_Z[n + 1])
                there = pl.ds((z + 8 - offset) % 8 * 2 + i, 8, stride=16)
                sum_a[there, :] = sum_a[there, :] + pltpu.roll(landed[at], y, 0)
                there = pl.ds((y + 8 - 4 * kk - n) % 8 * 16 + i, 8, stride=2)
                sum_b[there, :] = pltpu.roll(landed[16 + at], z, 0)
    out[...] = (sum_a[...] + sum_b[...]).T * (1.0 / out.shape[0])


def body(genotypes, covariates, traits, trait_weights):
    part, width = genotypes.shape
    count = 4 * part
    cov_count, trait_count = covariates.shape[1], traits.shape[1]
    f32, bf16, i32 = jnp.float32, jnp.bfloat16, jnp.int32
    dma = pltpu.SemaphoreType.DMA
    return pl.pallas_call(
        kernel,
        name="epistasis",
        out_shape=jax.ShapeDtypeStruct((width, 128), f32),
        in_specs=[pl.BlockSpec(memory_space=pl.ANY)] * 4,
        out_specs=pl.BlockSpec(memory_space=pltpu.VMEM),
        scratch_shapes=[
            pltpu.VMEM((A_SLOTS - 1, part, width), i32),
            pltpu.VMEM((A_SLOTS, 2, 2, part, width), i32),
            pltpu.VMEM((SIDE, 2, 2, part, width), i32),
            pltpu.VMEM((4, cov_count, part), f32),
            pltpu.VMEM((4, trait_count, part), f32),
            pltpu.SMEM((trait_count,), f32),
            pltpu.VMEM((count, 2 * count), bf16),
            pltpu.VMEM((count, count), f32),
            pltpu.VMEM((trait_count, count), f32),
            pltpu.VMEM(((A_SLOTS + SIDE) * count, 3 * count), bf16),
            pltpu.VMEM((3 * count, A_SLOTS * width), bf16),
            pltpu.VMEM((3 * count, SIDE * width), bf16),
            pltpu.VMEM((count, A_SLOTS * width), f32),
            pltpu.VMEM((count, SIDE * width), f32),
            pltpu.VMEM((2 * SIDE, 8, width), f32),
            pltpu.VMEM((32, 8, width), f32),
            pltpu.VMEM((128, width), f32),
            pltpu.VMEM((128, width), f32),
            dma((4,)), dma((4,)), dma((8,)), dma((SIDE,)), dma((SIDE,)), dma((SIDE,)),
            dma((A_SLOTS, 2)), dma((A_SLOTS,)), dma((A_SLOTS,)), dma((A_SLOTS,)),
            dma((2, 3)), dma((2, 3)), dma((3,)), dma((32,)), dma,
        ],
        compiler_params=pltpu.CompilerParams(
            collective_id=0, has_side_effects=True, vmem_limit_bytes=56 << 20
        ),
    )(genotypes, covariates.T, traits.T, trait_weights)


def solution(mesh):
    placed = (P("samp", "var"), P("samp", None), P("samp", None), P())
    return jax.shard_map(
        body, mesh=mesh, in_specs=placed, out_specs=P("var", None), check_vma=False
    )
```

```python
import math

import jax
import jax.numpy as jnp
from jax import lax
from jax.experimental import pallas as pl
from jax.experimental.pallas import tpu as pltpu
from jax.sharding import PartitionSpec as P

MESH = pl.DeviceIdType.MESH
HIGHEST = lax.Precision.HIGHEST
SIDE = 4
ALONG_Z = (0, 1, 2, -3, 4)
A_SLOTS = len(ALONG_Z)


def dot(a, b, contract=((1,), (0,)), precision=None):
    return lax.dot_general(
        a, b, (contract, ((), ())), precision=precision, preferred_element_type=jnp.float32
    )


def split(value):
    high = value.astype(jnp.bfloat16)
    return high, (value - high.astype(jnp.float32)).astype(jnp.bfloat16)


def sweep(matrix, begin, end):
    size = matrix.shape[0]
    rows = lax.broadcasted_iota(jnp.int32, (size, size), 0)
    cols = lax.broadcasted_iota(jnp.int32, (size, size), 1)
    for k in range(begin, end, 2):
        row_1, row_2 = matrix[k : k + 1, :], matrix[k + 1 : k + 2, :]
        col_1, col_2 = matrix[:, k : k + 1], matrix[:, k + 1 : k + 2]
        p, q, r = row_1[:, k : k + 1], row_1[:, k + 1 : k + 2], row_2[:, k + 1 : k + 2]
        scale = 1.0 / (p * r - q * q)
        row_1 = jnp.where(cols == k, -1.0, jnp.where(cols == k + 1, 0.0, row_1))
        row_2 = jnp.where(cols == k + 1, -1.0, jnp.where(cols == k, 0.0, row_2))
        col_1 = jnp.where(rows == k, -1.0, jnp.where(rows == k + 1, 0.0, col_1))
        col_2 = jnp.where(rows == k + 1, -1.0, jnp.where(rows == k, 0.0, col_2))
        kept = (rows == k) | (rows == k + 1) | (cols == k) | (cols == k + 1)
        matrix = (
            jnp.where(kept, 0.0, matrix)
            - col_1 * ((r * row_1 - q * row_2) * scale)
            - col_2 * ((p * row_2 - q * row_1) * scale)
        )
    return matrix


def kernel(
    geno, cov, trait, weights, out,
    unit, line, abuf, bbuf, covb, tw, pcat, qmat, ysc, hcat, rcat_a, rcat_b, rfull_a, rfull_b,
    tiles, landed, sum_a, sum_b,
    z_send, z_recv, y_send, y_recv, bx_send, bx_recv, ax_send, ax_recv, core_send, core_recv,
    small_send, small_recv, own_sem, out_send, out_recv,
):
    section = lax.axis_index("samp")
    block = lax.axis_index("var")
    l, k = section // 2, section % 2
    h, z, y = block % 2, (block // 2) % 8, block // 16
    same = (h == l).astype(jnp.int32)
    shift = same * k + (1 - same) * h

    def index(yy, zz, hh):
        return ((yy + 16) % 8 * 8 + (zz + 16) % 8) * 2 + hh

    def samp(ll, kk):
        return 2 * ll + kk

    def is_me(target):
        return (target[0] == section) & (target[1] == block)

    def unless_me(target, action):
        pl.when(jnp.logical_not(is_me(target)))(action)

    def send(src, dst, send_sem, recv_sem, target):
        return pltpu.make_async_remote_copy(
            src_ref=src, dst_ref=dst, send_sem=send_sem, recv_sem=recv_sem,
            device_id=target, device_id_type=MESH,
        )

    def send_or_copy(src, dst, send_sem, recv_sem, target):
        mine = is_me(target)
        remote = send(src, dst, send_sem, recv_sem, target)
        pl.when(jnp.logical_not(mine))(remote.start)
        pl.when(mine)(pltpu.make_async_copy(src, dst, recv_sem).start)
        return lambda: unless_me(target, remote.wait_send)

    def landing(ref, sem):
        pltpu.make_async_copy(ref, ref, sem).wait()

    own_part = covb.at[2 * k + l]
    own = [
        pltpu.make_async_copy(cov, own_part.at[: cov.shape[0]], own_sem.at[0]),
        pltpu.make_async_copy(trait, own_part.at[cov.shape[0] :], own_sem.at[1]),
        pltpu.make_async_copy(weights, tw, own_sem.at[2]),
        pltpu.make_async_copy(geno, unit, own_sem.at[3]),
    ]
    for copy in own:
        copy.start()

    peers = [((section + step) % 4, block) for step in range(1, 4)]
    z_targets = [(section, index(y, z - d, h)) for d in ALONG_Z[1:4]]
    z_sources = [(section, index(y, z + d, h)) for d in ALONG_Z[1:4]]
    y_offsets = (0, 1, 7, 2, 6, 3, 5)
    y_targets = {e: (samp(l, e // SIDE), index(y - e, z, h)) for e in y_offsets}
    y_onward = (samp(l, 1), index(y - 2 + 4 * k, z, h))
    z_onward = z_targets[1]
    y_sources = [
        (samp(l, kk), index(y + (4 * k + b if b else k * (2 - 4 * kk)), z, h))
        for b in range(SIDE)
        for kk in range(2)
    ]
    beside = (samp(1 - l, k), block)
    sibling = (samp(l, 1 - k), block)
    ax_targets = [(samp(h, k), index(y, z, hh)) for hh in range(2)]
    ax_sources = [(samp(ll, k), index(y, z, l)) for ll in range(2)]

    barrier = pltpu.get_barrier_semaphore()
    for source in peers + z_sources + y_sources + [beside, sibling] + ax_sources:
        unless_me(
            source,
            lambda source=source: pl.semaphore_signal(
                barrier, inc=1, device_id=source, device_id_type=MESH
            ),
        )
    for copy in own:
        copy.wait()
    pl.semaphore_wait(barrier, 18 - (1 - k) - same)

    sent = []
    small = []
    for n, peer in enumerate(peers):
        copy = send(own_part, own_part, small_send.at[n], small_recv.at[2 - n], peer)
        copy.start()
        small.append(copy)
    for n in range(3):
        copy = send(unit, line.at[n], z_send.at[n], z_recv.at[n], z_targets[n])
        copy.start()
        sent.append(copy.wait_send)
    for e in y_offsets:
        dst = bbuf.at[e % SIDE, k, l]
        sent.append(send_or_copy(unit, dst, y_send.at[e], y_recv.at[e % SIDE], y_targets[e]))

    def pass_a(slot):
        src = unit if slot == 0 else line.at[slot - 1]
        if slot > 0:
            landing(src, z_recv.at[slot - 1])
        for n, target in enumerate(ax_targets):
            dst = abuf.at[slot, k, l]
            sent.append(send_or_copy(src, dst, ax_send.at[slot, n], ax_recv.at[slot], target))
        if slot == 2:
            copy = send(src, line.at[3], z_send.at[3], z_recv.at[3], z_onward)
            copy.start()
            sent.append(copy.wait_send)

    b_order = (1 + 2 * k, 2, k, 3 - 3 * k)

    def pass_b(step):
        slot = b_order[step]
        half = bbuf.at[slot, :, l]
        landing(half, y_recv.at[slot])
        copy = send(half, half, bx_send.at[step], bx_recv.at[slot], beside)
        copy.start()
        sent.append(copy.wait_send)
        if step == 1:
            copy = send(bbuf.at[2, k, l], bbuf.at[0, k, l], y_send.at[4], y_recv.at[0], y_onward)
            copy.start()
            sent.append(copy.wait_send)

    def pass_core(slot):
        part = abuf.at[slot, k]
        landing(part, ax_recv.at[slot])
        copy = send(part, part, core_send.at[slot], core_recv.at[slot], sibling)
        copy.start()
        sent.append(copy.wait_send)

    pass_a(0)
    for copy in small:
        copy.wait()
    both = jnp.concatenate([covb[n] for n in range(4)], axis=1)
    cov_t, trait_t = both[: cov.shape[0]], both[cov.shape[0] :]
    width, count = cov_t.shape
    eye = (
        lax.broadcasted_iota(jnp.int32, (width, width), 0)
        == lax.broadcasted_iota(jnp.int32, (width, width), 1)
    ).astype(jnp.float32)
    swept = dot(cov_t, cov_t, ((1,), (1,)), HIGHEST) + count / 10.0 * eye
    pass_a(1)
    pass_b(0)
    pass_a(2)
    pass_b(1)
    swept = sweep(swept, 0, 12)
    pass_core(0)
    pass_b(2)
    swept = sweep(swept, 12, 20)
    pass_a(3)
    pass_core(1)
    swept = sweep(swept, 20, 28)
    pass_core(2)
    pass_a(4)
    swept = sweep(swept, 28, width)
    pass_b(3)
    pass_core(3)
    solved = dot(-swept, cov_t, precision=HIGHEST)
    hat = dot(cov_t, solved, ((0,), (0,)), HIGHEST)
    diagonal = lax.broadcasted_iota(jnp.int32, (count, count), 0) == lax.broadcasted_iota(
        jnp.int32, (count, count), 1
    )
    project = jnp.where(diagonal, 1.0, 0.0) - hat
    high, low = split(project)
    pcat[:, :count] = high
    pcat[:, count:] = low
    scaled = dot(trait_t, project, precision=HIGHEST) * (1.0 / math.sqrt(count))
    ysc[...] = scaled
    traits_id = lax.broadcasted_iota(jnp.int32, (scaled.shape[0], 1), 0)
    tw_col = sum(jnp.where(traits_id == t, tw[t], 0.0) for t in range(scaled.shape[0]))
    qmat[...] = dot(scaled * tw_col, scaled, ((0,), (0,)), HIGHEST)
    def prepare(genotypes, ats, rcat, rfull, hrows):
        genotypes = [g.astype(jnp.float32).reshape(count, 128) for g in genotypes]
        centred = (jnp.concatenate(genotypes, axis=1) - 1.0).astype(jnp.bfloat16)
        resids = dot(pcat[...], jnp.concatenate([centred, centred], axis=0))
        for n, (at, hrow) in enumerate(zip(ats, hrows)):
            resid = resids[:, n * 128 : (n + 1) * 128]
            high, low = split(resid)
            at = pl.ds(pl.multiple_of(at * 128, 128), 128)
            rfull[:, at] = 2.0 * resid - high.astype(jnp.float32)
            rcat[:count, at] = high
            rcat[count:, at] = high
            gram = dot(
                jnp.concatenate([high, low + low], axis=1),
                jnp.concatenate([high, high], axis=1),
                ((1,), (1,)),
            )
            h_high, h_low = split(gram * qmat[...])
            rows = pl.ds(pl.multiple_of(hrow * count, count), count)
            hcat[rows, :count] = h_high
            hcat[rows, count:] = h_low

    def prepare_b(first):
        slots = [first, first + 1]
        for slot in slots:
            landing(bbuf.at[slot, :, 1 - l], bx_recv.at[slot])
        hrows = [A_SLOTS + slot for slot in slots]
        prepare([bbuf[slot] for slot in slots], slots, rcat_b, rfull_b, hrows)

    def prepare_a(*slots):
        for slot in slots:
            landing(abuf.at[slot, 1 - k], core_recv.at[slot])
        prepare([abuf[slot] for slot in slots], slots, rcat_a, rfull_a, slots)

    def pairs(hrow, number, rcat, rfull, at):
        at = pl.ds(pl.multiple_of(at * 128, 128), 256)
        rows = pl.ds(pl.multiple_of(hrow * count, count), number * count)
        product = dot(hcat[rows, :], rcat[:, at])
        weighted = product.reshape(number, count, 256) * rfull[:, at][None]
        sums = jnp.sum(weighted, axis=1)
        return jnp.concatenate([sums, jnp.zeros((8 - number, 256), jnp.float32)], axis=0)

    row_ids = lax.broadcasted_iota(jnp.int32, (8, 128), 0)

    def give_back(slot):
        if slot < SIDE:
            offset = jnp.where(shift == 0, ALONG_Z[slot], ALONG_Z[slot + 1])
            owner, at, kind = index(y, z + offset, l), h * 8 + k * 4 + slot, 0
        else:
            owner, at, kind = index(y + 4 * k + slot - SIDE, z, h), 16 + l * 8 + k * 4 + slot - SIDE, 1
        for q in range(4):
            sem = out_send.at[slot * 4 + q]
            sent.append(
                send_or_copy(tiles.at[slot], landed.at[at], sem, out_recv.at[kind], (q, owner))
            )

    def score_a(part):
        sums = pltpu.roll(pairs(A_SLOTS, SIDE, rcat_a, rfull_a, shift + 2 * part), 4 * k, 0)
        tiles[2 * part] = sums[:, :128]
        tiles[2 * part + 1] = sums[:, 128:]

    def score_b(part, of_a):
        sums = pairs(shift + 2 * of_a, 2, rcat_b, rfull_b, 2 * part)
        sums = pltpu.roll(sums, shift + 2 * of_a, 0)
        picked = [sums[a : a + 1] for a in (0, 1, 2, 5, 4, 3, 6, 7)]
        sums = jnp.concatenate(picked, axis=0)
        for n in range(2):
            at, half = SIDE + 2 * part + n, sums[:, n * 128 : (n + 1) * 128]
            tiles[at] = tiles[at] + half if of_a else half

    prepare_b(2 * k)
    prepare_a(0, 1)
    pass_core(4)
    prepare_b(2 - 2 * k)
    prepare_a(2)
    score_a(0)

    @pl.when((same == 1) & (k == 0))
    def _():
        resid = 0.5 * (rfull_a[:, :128] + rcat_a[:count, :128].astype(jnp.float32))
        diag = dot(ysc[...], resid * resid, precision=HIGHEST)
        diag = jnp.sum(diag * diag * tw_col, axis=0, keepdims=True)
        tiles[0] = tiles[0] - jnp.where(row_ids == 0, diag, 0.0)

    give_back(1)
    give_back(0)
    score_b(0, 0)
    score_b(1, 0)
    prepare_a(3, 4)
    score_a(1)
    give_back(3)
    give_back(2)
    score_b(1, 1)
    give_back(7)
    give_back(6)
    score_b(0, 1)

    @pl.when(same == 1)
    def _():
        rows = pl.ds(pl.multiple_of((1 - k) * 4 * count, count), count)
        product = dot(hcat[rows, :], rcat_b[:, :128])
        extra = jnp.sum(product * rfull_b[:, :128], axis=0, keepdims=True)
        tile = jnp.where(row_ids == 4 * k, 0.0, tiles[SIDE])
        tiles[SIDE] = jnp.where(row_ids == 4 * (1 - k), extra, tile)

    give_back(4)
    give_back(5)

    sum_a[...] = jnp.zeros_like(sum_a)
    landing(landed.at[:16], out_recv.at[0])
    for i in range(2):
        mixed = jnp.not_equal(h, i).astype(jnp.int32)
        for kk in range(2):
            first = mixed * (1 - h) + (1 - mixed) * kk
            for n in range(SIDE):
                offset = jnp.where(first == 0, ALONG_Z[n], ALONG_Z[n + 1])
                there = pl.ds((z + 8 - offset) % 8 * 2 + i, 8, stride=16)
                sum_a[there, :] = sum_a[there, :] + pltpu.roll(landed[i * 8 + kk * 4 + n], y, 0)
    landing(landed.at[16:], out_recv.at[1])
    for i in range(2):
        for e in range(8):
            there = pl.ds((y + 8 - e) % 8 * 16 + i, 8, stride=2)
            sum_b[there, :] = pltpu.roll(landed[16 + i * 8 + e], z, 0)
    for wait in sent:
        wait()
    out[...] = (sum_a[...] + sum_b[...]).T * (1.0 / out.shape[0])


def body(genotypes, covariates, traits, trait_weights):
    part, width = genotypes.shape
    count = 4 * part
    cov_count, trait_count = covariates.shape[1], traits.shape[1]
    f32, bf16, i32 = jnp.float32, jnp.bfloat16, jnp.int32
    dma = pltpu.SemaphoreType.DMA
    inputs = (genotypes, covariates.T, traits.T, trait_weights)
    held = [pltpu.with_memory_space_constraint(value, pltpu.HBM) for value in inputs]
    return pl.pallas_call(
        kernel,
        name="epistasis",
        out_shape=jax.ShapeDtypeStruct((width, 128), f32),
        in_specs=[pl.BlockSpec(memory_space=pl.ANY)] * 4,
        out_specs=pl.BlockSpec(memory_space=pltpu.VMEM),
        scratch_shapes=[
            pltpu.VMEM((part, width), i32),
            pltpu.VMEM((A_SLOTS - 1, part, width), i32),
            pltpu.VMEM((A_SLOTS, 2, 2, part, width), i32),
            pltpu.VMEM((SIDE, 2, 2, part, width), i32),
            pltpu.VMEM((4, cov_count + trait_count, part), f32),
            pltpu.SMEM((trait_count,), f32),
            pltpu.VMEM((count, 2 * count), bf16),
            pltpu.VMEM((count, count), f32),
            pltpu.VMEM((trait_count, count), f32),
            pltpu.VMEM(((A_SLOTS + SIDE) * count, 2 * count), bf16),
            pltpu.VMEM((2 * count, A_SLOTS * width), bf16),
            pltpu.VMEM((2 * count, SIDE * width), bf16),
            pltpu.VMEM((count, A_SLOTS * width), f32),
            pltpu.VMEM((count, SIDE * width), f32),
            pltpu.VMEM((2 * SIDE, 8, width), f32),
            pltpu.VMEM((32, 8, width), f32),
            pltpu.VMEM((128, width), f32),
            pltpu.VMEM((128, width), f32),
            dma((4,)), dma((4,)), dma((8,)), dma((SIDE,)), dma((SIDE,)), dma((SIDE,)),
            dma((A_SLOTS, 2)), dma((A_SLOTS,)), dma((A_SLOTS,)), dma((A_SLOTS,)),
            dma((3,)), dma((3,)), dma((4,)), dma((32,)), dma((2,)),
        ],
        compiler_params=pltpu.CompilerParams(
            collective_id=0, has_side_effects=True, vmem_limit_bytes=32 << 20
        ),
    )(*held)


def solution(mesh):
    placed = (P("samp", "var"), P("samp", None), P("samp", None), P())
    return jax.shard_map(
        body, mesh=mesh, in_specs=placed, out_specs=P("var", None), check_vma=False
    )
```

```python
import math

import jax
import jax.numpy as jnp
from jax import lax
from jax.experimental import pallas as pl
from jax.experimental.pallas import tpu as pltpu
from jax.sharding import PartitionSpec as P

MESH = pl.DeviceIdType.MESH
HIGHEST = lax.Precision.HIGHEST
SIDE = 4
ALONG_Z = (0, -1, -2, 3, 4)
A_SLOTS = len(ALONG_Z)


def dot(a, b, contract=((1,), (0,)), precision=None):
    return lax.dot_general(
        a, b, (contract, ((), ())), precision=precision, preferred_element_type=jnp.float32
    )


def split(value):
    high = value.astype(jnp.bfloat16)
    return high, (value - high.astype(jnp.float32)).astype(jnp.bfloat16)


def sweep(matrix, begin, end):
    size = matrix.shape[0]
    rows = lax.broadcasted_iota(jnp.int32, (size, size), 0)
    cols = lax.broadcasted_iota(jnp.int32, (size, size), 1)
    for k in range(begin, end, 2):
        row_1, row_2 = matrix[k : k + 1, :], matrix[k + 1 : k + 2, :]
        col_1 = jnp.broadcast_to(matrix[:, k : k + 1], (size, size))
        col_2 = jnp.broadcast_to(matrix[:, k + 1 : k + 2], (size, size))
        p, q, r = col_1[k : k + 1, :], col_2[k : k + 1, :], col_2[k + 1 : k + 2, :]
        scale = 1.0 / (p * r - q * q)
        row_1 = jnp.where(cols[:1] == k, -1.0, jnp.where(cols[:1] == k + 1, 0.0, row_1))
        row_2 = jnp.where(cols[:1] == k + 1, -1.0, jnp.where(cols[:1] == k, 0.0, row_2))
        col_1 = jnp.where(rows == k, -1.0, jnp.where(rows == k + 1, 0.0, col_1))
        col_2 = jnp.where(rows == k + 1, -1.0, jnp.where(rows == k, 0.0, col_2))
        kept = (rows == k) | (rows == k + 1) | (cols == k) | (cols == k + 1)
        matrix = (
            jnp.where(kept, 0.0, matrix)
            - col_1 * ((r * row_1 - q * row_2) * scale)
            - col_2 * ((p * row_2 - q * row_1) * scale)
        )
    return matrix


def kernel(
    geno, cov, trait, weights, out,
    unit, line, abuf, bbuf, covb, tw, pcat, qmat, ysc, hcat, rcat_a, rcat_b, rfull_a, rfull_b,
    tiles, landed, sum_a, sum_b,
    z_send, z_recv, y_send, y_recv, bx_send, bx_recv, ax_send, ax_recv, core_send, core_recv,
    small_send, small_recv, own_sem, out_send, out_recv,
):
    section = lax.axis_index("samp")
    block = lax.axis_index("var")
    l, k = section // 2, section % 2
    h, z, y = block % 2, (block // 2) % 8, block // 16
    same = (h == l).astype(jnp.int32)
    shift = same * k + (1 - same) * h

    def index(yy, zz, hh):
        return (lax.rem(yy + 16, 8) * 8 + lax.rem(zz + 16, 8)) * 2 + hh

    def samp(ll, kk):
        return 2 * ll + kk

    def is_me(target):
        return (target[0] == section) & (target[1] == block)

    def unless_me(target, action):
        pl.when(jnp.logical_not(is_me(target)))(action)

    def send(src, dst, send_sem, recv_sem, target):
        return pltpu.make_async_remote_copy(
            src_ref=src, dst_ref=dst, send_sem=send_sem, recv_sem=recv_sem,
            device_id=target, device_id_type=MESH,
        )

    def send_or_copy(src, dst, send_sem, recv_sem, target):
        mine = is_me(target)
        remote = send(src, dst, send_sem, recv_sem, target)
        pl.when(jnp.logical_not(mine))(remote.start)
        pl.when(mine)(pltpu.make_async_copy(src, dst, recv_sem).start)
        return lambda: unless_me(target, remote.wait_send)

    def send_on(src, dst, send_sem, recv_sem, target):
        remote = send(src, dst, send_sem, recv_sem, target)
        remote.start()
        return remote.wait_send

    def landing(ref, sem):
        pltpu.make_async_copy(ref, ref, sem).wait()

    own_part = covb.at[2 * k + l]
    own = [
        pltpu.make_async_copy(cov, own_part.at[: cov.shape[0]], own_sem.at[0]),
        pltpu.make_async_copy(trait, own_part.at[cov.shape[0] :], own_sem.at[1]),
        pltpu.make_async_copy(weights, tw, own_sem.at[2]),
        pltpu.make_async_copy(geno, unit, own_sem.at[3]),
    ]
    for copy in own:
        copy.start()

    peers = [((section + step) % 4, block) for step in range(1, 4)]
    z_targets = [(section, index(y, z - d, h)) for d in ALONG_Z[2:4]]
    z_sources = [(section, index(y, z + d, h)) for d in ALONG_Z[2:4]]
    a1_targets = [(samp(h, k), index(y, z - ALONG_Z[1], hh)) for hh in range(2)]
    a1_sources = [(samp(ll, k), index(y, z + ALONG_Z[1], l)) for ll in range(2)]
    y_across = {e: (samp(1 - l, e // SIDE), index(y - e, z, h)) for e in (0, 1, 7)}
    y_across_sources = [(samp(1 - l, kk), index(y + 7 * k, z, h)) for kk in range(2)]
    y_across_core_0 = [(samp(1 - l, kk), index(y + 1, z, h)) for kk in range(2)]
    y_offsets = (0, 1, 7, 2, 6, 3, 5)
    y_targets = {e: (samp(l, e // SIDE), index(y - e, z, h)) for e in y_offsets}
    y_onward = (samp(l, 1), index(y - 2 + 4 * k, z, h))
    z_onward = z_targets[0]
    y_sources = [
        (samp(l, kk), index(y + (4 * k + b if b else k * (2 - 4 * kk)), z, h))
        for b in range(SIDE)
        for kk in range(2)
    ]
    beside = (samp(1 - l, k), block)
    sibling = (samp(l, 1 - k), block)
    ax_targets = [(samp(h, k), index(y, z, hh)) for hh in range(2)]
    ax_sources = [(samp(ll, k), index(y, z, l)) for ll in range(2)]
    a4_across = [(samp(h, 1 - k), index(y, z, hh)) for hh in range(2)]
    a4_across_sources = [(samp(ll, 1 - k), index(y, z, l)) for ll in range(2)]

    owners = []
    for slot in range(SIDE):
        offset = jnp.where(shift == 0, ALONG_Z[slot], ALONG_Z[slot + 1])
        owners.append((index(y, z + offset, l), h * 8 + k * 4 + slot))
    for slot in range(SIDE):
        owners.append((index(y + 4 * k + slot, z, h), 16 + l * 8 + k * 4 + slot))

    barrier = pltpu.get_barrier_semaphore()
    for source in peers + z_sources + y_sources[1:] + [beside, sibling] + a4_across_sources + (
        a1_sources + y_across_sources
    ):
        pl.semaphore_signal(barrier, inc=1, device_id=source, device_id_type=MESH)
    for source in y_across_core_0:
        pl.when(k == 0)(
            lambda source=source: pl.semaphore_signal(
                barrier, inc=1, device_id=source, device_id_type=MESH
            )
        )
    for source in [y_sources[0]] + ax_sources:
        unless_me(
            source,
            lambda source=source: pl.semaphore_signal(
                barrier, inc=1, device_id=source, device_id_type=MESH
            ),
        )
    for copy in own:
        copy.wait()
    pl.semaphore_wait(barrier, 24 - (1 - k) - same)

    sent = []
    small = []
    for n, peer in enumerate(peers):
        copy = send(own_part, own_part, small_send.at[n], small_recv.at[2 - n], peer)
        copy.start()
        small.append(copy)

    def send_y(e):
        slot = e % SIDE
        deliver = send_or_copy if e == 0 else send_on
        dst = bbuf.at[slot, k, l]
        sent.append(deliver(unit, dst, y_send.at[e], y_recv.at[slot], y_targets[e]))
        if e in y_across:
            sem = y_send.at[8 + e]
            sent.append(send_on(unit, dst, sem, bx_recv.at[slot], y_across[e]))

    def send_z(n):
        sem = z_send.at[n]
        sent.append(send_on(unit, line.at[n], sem, z_recv.at[n], z_targets[n - 1]))

    def send_slot(slot, targets):
        for n, target in enumerate(targets):
            deliver = send_or_copy if slot == 0 else send_on
            dst, sem = abuf.at[slot, k, l], ax_send.at[slot, n]
            sent.append(deliver(unit, dst, sem, ax_recv.at[slot], target))

    send_y(1)
    send_y(7)
    send_slot(1, a1_targets)
    send_slot(0, ax_targets)
    send_z(1)
    send_y(2)
    send_y(6)
    send_y(0)
    send_z(2)
    send_y(3)
    send_y(5)

    def pass_a(slot):
        src = line.at[slot - 1]
        landing(src, z_recv.at[slot - 1])
        for n, target in enumerate(ax_targets):
            dst = abuf.at[slot, k, l]
            sent.append(send_or_copy(src, dst, ax_send.at[slot, n], ax_recv.at[slot], target))
            if slot == 4:
                sem, sem_there = ax_send.at[slot, 2 + n], core_recv.at[slot]
                sent.append(send_on(src, dst, sem, sem_there, a4_across[n]))
        if slot == 2:
            copy = send(src, line.at[3], z_send.at[3], z_recv.at[3], z_onward)
            copy.start()
            sent.append(copy.wait_send)

    b_order = (1 + 2 * k, 2, k, 3 - 3 * k)

    def pass_b(step):
        slot = b_order[step]
        half = bbuf.at[slot, :, l]
        landing(half, y_recv.at[slot])
        if step == 0:
            return
        copy = send(half, half, bx_send.at[step], bx_recv.at[slot], beside)
        if step == 2:
            pl.when(k == 1)(copy.start)
            sent.append(lambda: pl.when(k == 1)(copy.wait_send))
        else:
            copy.start()
            sent.append(copy.wait_send)
        if step == 1:
            copy = send(bbuf.at[2, k, l], bbuf.at[0, k, l], y_send.at[4], y_recv.at[0], y_onward)
            copy.start()
            sent.append(copy.wait_send)

    def pass_core(slot):
        part = abuf.at[slot, k]
        landing(part, ax_recv.at[slot])
        copy = send(part, part, core_send.at[slot], core_recv.at[slot], sibling)
        copy.start()
        sent.append(copy.wait_send)

    for copy in small:
        copy.wait()
    both = jnp.concatenate([covb[n] for n in range(4)], axis=1)
    cov_t, trait_t = both[: cov.shape[0]], both[cov.shape[0] :]
    width, count = cov_t.shape
    eye = (
        lax.broadcasted_iota(jnp.int32, (width, width), 0)
        == lax.broadcasted_iota(jnp.int32, (width, width), 1)
    ).astype(jnp.float32)
    swept = dot(cov_t, cov_t, ((1,), (1,)), HIGHEST) + count / 10.0 * eye
    pass_a(2)
    pass_b(1)
    swept = sweep(swept, 0, 20)
    pass_core(0)
    pass_b(2)
    pass_a(3)
    pass_core(1)
    swept = sweep(swept, 20, width)
    pass_core(2)
    pass_b(0)
    solved = dot(-swept, cov_t, precision=HIGHEST)
    hat = dot(cov_t, solved, ((0,), (0,)), HIGHEST)
    diagonal = lax.broadcasted_iota(jnp.int32, (count, count), 0) == lax.broadcasted_iota(
        jnp.int32, (count, count), 1
    )
    project = jnp.where(diagonal, 1.0, 0.0) - hat
    high, low = split(project)
    pcat[:, :count] = high
    pcat[:, count:] = low
    pass_a(4)
    pass_b(3)
    scaled = dot(trait_t, project, precision=HIGHEST) * (1.0 / math.sqrt(count))
    ysc[...] = scaled
    traits_id = lax.broadcasted_iota(jnp.int32, (scaled.shape[0], 1), 0)
    tw_col = sum(jnp.where(traits_id == t, tw[t], 0.0) for t in range(scaled.shape[0]))
    qmat[...] = dot(scaled * tw_col, scaled, ((0,), (0,)), HIGHEST)
    pass_core(3)
    def prepare(genotypes, ats, rcat, rfull, hrows):
        genotypes = [g.astype(jnp.float32).reshape(count, 128) for g in genotypes]
        centred = (jnp.concatenate(genotypes, axis=1) - 1.0).astype(jnp.bfloat16)
        resids = dot(pcat[...], jnp.concatenate([centred, centred], axis=0))
        for n, (at, hrow) in enumerate(zip(ats, hrows)):
            resid = resids[:, n * 128 : (n + 1) * 128]
            high, low = split(resid)
            at = pl.ds(pl.multiple_of(at * 128, 128), 128)
            rfull[:, at] = 2.0 * resid - high.astype(jnp.float32)
            rcat[:count, at] = high
            rcat[count:, at] = high
            gram = dot(
                jnp.concatenate([high, low + low], axis=1),
                jnp.concatenate([high, high], axis=1),
                ((1,), (1,)),
            )
            h_high, h_low = split(gram * qmat[...])
            rows = pl.ds(pl.multiple_of(hrow * count, count), count)
            hcat[rows, :count] = h_high
            hcat[rows, count:] = h_low

    def prepare_b(first):
        slots = [first, first + 1]
        for slot in slots:
            landing(bbuf.at[slot, :, 1 - l], bx_recv.at[slot])
        hrows = [A_SLOTS + slot for slot in slots]
        prepare([bbuf[slot] for slot in slots], slots, rcat_b, rfull_b, hrows)

    def prepare_a(*slots):
        for slot in slots:
            if slot == 4:
                landing(abuf.at[slot, k], ax_recv.at[slot])
            landing(abuf.at[slot, 1 - k], core_recv.at[slot])
        prepare([abuf[slot] for slot in slots], slots, rcat_a, rfull_a, slots)

    def pairs(hrow, number, rcat, rfull, at):
        at = pl.ds(pl.multiple_of(at * 128, 128), 256)
        rows = pl.ds(pl.multiple_of(hrow * count, count), number * count)
        product = dot(hcat[rows, :], rcat[:, at])
        weighted = product.reshape(number, count, 256) * rfull[:, at][None]
        sums = jnp.sum(weighted, axis=1)
        return jnp.concatenate([sums, jnp.zeros((8 - number, 256), jnp.float32)], axis=0)

    row_ids = lax.broadcasted_iota(jnp.int32, (8, 128), 0)

    def give_back(slot):
        owner, at = owners[slot]
        for q in range(4):
            sem = out_send.at[slot * 4 + q]
            deliver = send_or_copy if slot in (0, SIDE) else send_on
            kind = out_recv.at[slot // SIDE]
            sent.append(deliver(tiles.at[slot], landed.at[at], sem, kind, (q, owner)))

    near, rest = 2 * k, 2 - 2 * k

    def add(at, part, fresh):
        tiles[at] = part if fresh else tiles[at] + part

    def score_a(part, number, first, fresh):
        sums = pairs(A_SLOTS + first, number, rcat_a, rfull_a, shift + 2 * part)
        sums = pltpu.roll(sums, 4 * k + first, 0)
        add(2 * part, sums[:, :128], fresh)
        add(2 * part + 1, sums[:, 128:], fresh)

    def score_b(first, of_a, number, fresh):
        sums = pairs(shift + 2 * of_a, number, rcat_b, rfull_b, first)
        sums = pltpu.roll(sums, shift + 2 * of_a, 0)
        picked = [sums[a : a + 1] for a in (0, 5, 6, 3, 4, 7, 2, 1)]
        sums = jnp.concatenate(picked, axis=0)
        add(SIDE + first, sums[:, :128], fresh)
        add(SIDE + first + 1, sums[:, 128:], fresh)

    prepare_b(near)
    prepare_a(0, 1)
    prepare_a(2)
    score_a(0, 2, near, True)
    score_b(near, 0, 2, True)
    prepare_b(rest)
    score_a(0, 2, rest, False)
    score_b(rest, 0, 2, True)

    @pl.when((same == 1) & (k == 0))
    def _():
        resid = 0.5 * (rfull_a[:, :128] + rcat_a[:count, :128].astype(jnp.float32))
        diag = dot(ysc[...], resid * resid, precision=HIGHEST)
        diag = jnp.sum(diag * diag * tw_col, axis=0, keepdims=True)
        tiles[0] = tiles[0] - jnp.where(row_ids == 0, diag, 0.0)

    give_back(1)
    give_back(0)
    prepare_a(3, 4)
    score_a(1, 4, 0, True)
    give_back(3)
    give_back(2)
    score_b(2, 1, 2, False)
    give_back(7)
    give_back(6)
    score_b(0, 1, 2, False)

    @pl.when(same == 1)
    def _():
        rows = pl.ds(pl.multiple_of((1 - k) * 4 * count, count), count)
        product = dot(hcat[rows, :], rcat_b[:, :128])
        extra = jnp.sum(product * rfull_b[:, :128], axis=0, keepdims=True)
        tile = jnp.where(row_ids == 4 * k, 0.0, tiles[SIDE])
        tiles[SIDE] = jnp.where(row_ids == 4 * (1 - k), extra, tile)

    give_back(4)
    give_back(5)

    sum_a[...] = jnp.zeros_like(sum_a)
    for wait in sent:
        wait()
    landing(landed.at[:16], out_recv.at[0])
    for i in range(2):
        mixed = jnp.not_equal(h, i).astype(jnp.int32)
        for kk in range(2):
            first = mixed * (1 - h) + (1 - mixed) * kk
            for n in range(SIDE):
                offset = jnp.where(first == 0, ALONG_Z[n], ALONG_Z[n + 1])
                there = pl.ds((z + 8 - offset) % 8 * 2 + i, 8, stride=16)
                sum_a[there, :] = sum_a[there, :] + pltpu.roll(landed[i * 8 + kk * 4 + n], y, 0)
    landing(landed.at[16:], out_recv.at[1])
    for i in range(2):
        for e in range(8):
            there = pl.ds((y + 8 - e) % 8 * 16 + i, 8, stride=2)
            sum_b[there, :] = pltpu.roll(landed[16 + i * 8 + e], z, 0)
    out[...] = (sum_a[...] + sum_b[...]).T * (1.0 / out.shape[0])


def body(genotypes, covariates, traits, trait_weights):
    part, width = genotypes.shape
    count = 4 * part
    cov_count, trait_count = covariates.shape[1], traits.shape[1]
    f32, bf16, i32 = jnp.float32, jnp.bfloat16, jnp.int32
    dma = pltpu.SemaphoreType.DMA
    inputs = (genotypes, covariates.T, traits.T, trait_weights)
    held = [pltpu.with_memory_space_constraint(value, pltpu.HBM) for value in inputs]
    return pl.pallas_call(
        kernel,
        name="epistasis",
        out_shape=jax.ShapeDtypeStruct((width, 128), f32),
        in_specs=[pl.BlockSpec(memory_space=pl.ANY)] * 4,
        out_specs=pl.BlockSpec(memory_space=pltpu.VMEM),
        scratch_shapes=[
            pltpu.VMEM((part, width), i32),
            pltpu.VMEM((A_SLOTS - 1, part, width), i32),
            pltpu.VMEM((A_SLOTS, 2, 2, part, width), i32),
            pltpu.VMEM((SIDE, 2, 2, part, width), i32),
            pltpu.VMEM((4, cov_count + trait_count, part), f32),
            pltpu.SMEM((trait_count,), f32),
            pltpu.VMEM((count, 2 * count), bf16),
            pltpu.VMEM((count, count), f32),
            pltpu.VMEM((trait_count, count), f32),
            pltpu.VMEM(((A_SLOTS + SIDE) * count, 2 * count), bf16),
            pltpu.VMEM((2 * count, A_SLOTS * width), bf16),
            pltpu.VMEM((2 * count, SIDE * width), bf16),
            pltpu.VMEM((count, A_SLOTS * width), f32),
            pltpu.VMEM((count, SIDE * width), f32),
            pltpu.VMEM((2 * SIDE, 8, width), f32),
            pltpu.VMEM((32, 8, width), f32),
            pltpu.VMEM((128, width), f32),
            pltpu.VMEM((128, width), f32),
            dma((4,)), dma((4,)), dma((16,)), dma((SIDE,)), dma((SIDE,)), dma((SIDE,)),
            dma((A_SLOTS, 4)), dma((A_SLOTS,)), dma((A_SLOTS,)), dma((A_SLOTS,)),
            dma((3,)), dma((3,)), dma((4,)), dma((32,)), dma((2,)),
        ],
        compiler_params=pltpu.CompilerParams(
            collective_id=0, has_side_effects=True, vmem_limit_bytes=32 << 20
        ),
    )(*held)


def solution(mesh):
    placed = (P("samp", "var"), P("samp", None), P("samp", None), P())
    return jax.shard_map(
        body, mesh=mesh, in_specs=placed, out_specs=P("var", None), check_vma=False
    )
```

```python
import math

import jax
import jax.numpy as jnp
from jax import lax
from jax.experimental import pallas as pl
from jax.experimental.pallas import tpu as pltpu
from jax.sharding import PartitionSpec as P

MESH = pl.DeviceIdType.MESH
HIGHEST = lax.Precision.HIGHEST
SIDE = 4
ALONG_Z = (0, -1, -2, 3, 4)
A_SLOTS = len(ALONG_Z)


def dot(a, b, contract=((1,), (0,)), precision=None):
    return lax.dot_general(
        a, b, (contract, ((), ())), precision=precision, preferred_element_type=jnp.float32
    )


def split(value):
    high = value.astype(jnp.bfloat16)
    return high, (value - high.astype(jnp.float32)).astype(jnp.bfloat16)


def sweep(matrix, begin, end):
    size = matrix.shape[0]
    rows = lax.broadcasted_iota(jnp.int32, (size, size), 0)
    cols = lax.broadcasted_iota(jnp.int32, (size, size), 1)
    for k in range(begin, end, 2):
        row_1, row_2 = matrix[k : k + 1, :], matrix[k + 1 : k + 2, :]
        col_1 = jnp.broadcast_to(matrix[:, k : k + 1], (size, size))
        col_2 = jnp.broadcast_to(matrix[:, k + 1 : k + 2], (size, size))
        p, q, r = col_1[k : k + 1, :], col_2[k : k + 1, :], col_2[k + 1 : k + 2, :]
        scale = 1.0 / (p * r - q * q)
        row_1 = jnp.where(cols[:1] == k, -1.0, jnp.where(cols[:1] == k + 1, 0.0, row_1))
        row_2 = jnp.where(cols[:1] == k + 1, -1.0, jnp.where(cols[:1] == k, 0.0, row_2))
        col_1 = jnp.where(rows == k, -1.0, jnp.where(rows == k + 1, 0.0, col_1))
        col_2 = jnp.where(rows == k + 1, -1.0, jnp.where(rows == k, 0.0, col_2))
        kept = (rows == k) | (rows == k + 1) | (cols == k) | (cols == k + 1)
        matrix = (
            jnp.where(kept, 0.0, matrix)
            - col_1 * ((r * row_1 - q * row_2) * scale)
            - col_2 * ((p * row_2 - q * row_1) * scale)
        )
    return matrix


def kernel(
    geno, cov, trait, weights, out,
    unit, line, abuf, bbuf, covb, tw, pcat, qmat, ysc, hcat, rcat_a, rcat_b, rfull_a, rfull_b,
    tiles, landed, sum_a, sum_b,
    z_send, z_recv, y_send, y_recv, bx_send, bx_recv, ax_send, ax_recv, core_send, core_recv,
    small_send, small_recv, own_sem, out_send, out_recv,
):
    section = lax.axis_index("samp")
    block = lax.axis_index("var")
    l, k = section // 2, section % 2
    h, z, y = block % 2, (block // 2) % 8, block // 16
    same = (h == l).astype(jnp.int32)
    shift = same * k + (1 - same) * h

    def index(yy, zz, hh):
        return (lax.rem(yy + 16, 8) * 8 + lax.rem(zz + 16, 8)) * 2 + hh

    def samp(ll, kk):
        return 2 * ll + kk

    def is_me(target):
        return (target[0] == section) & (target[1] == block)

    def unless_me(target, action):
        pl.when(jnp.logical_not(is_me(target)))(action)

    def send(src, dst, send_sem, recv_sem, target):
        return pltpu.make_async_remote_copy(
            src_ref=src, dst_ref=dst, send_sem=send_sem, recv_sem=recv_sem,
            device_id=target, device_id_type=MESH,
        )

    def send_or_copy(src, dst, send_sem, recv_sem, target):
        mine = is_me(target)
        remote = send(src, dst, send_sem, recv_sem, target)
        pl.when(jnp.logical_not(mine))(remote.start)
        pl.when(mine)(pltpu.make_async_copy(src, dst, recv_sem).start)
        return lambda: unless_me(target, remote.wait_send)

    def send_on(src, dst, send_sem, recv_sem, target):
        remote = send(src, dst, send_sem, recv_sem, target)
        remote.start()
        return remote.wait_send

    def landing(ref, sem):
        pltpu.make_async_copy(ref, ref, sem).wait()

    own_part = covb.at[2 * k + l]
    own = [
        pltpu.make_async_copy(cov, own_part.at[: cov.shape[0]], own_sem.at[0]),
        pltpu.make_async_copy(trait, own_part.at[cov.shape[0] :], own_sem.at[1]),
        pltpu.make_async_copy(weights, tw, own_sem.at[2]),
        pltpu.make_async_copy(geno, unit, own_sem.at[3]),
    ]
    for copy in own:
        copy.start()

    peers = [((section + step) % 4, block) for step in range(1, 4)]
    z_targets = [(section, index(y, z - d, h)) for d in ALONG_Z[2:4]]
    z_sources = [(section, index(y, z + d, h)) for d in ALONG_Z[2:4]]
    a1_targets = [(samp(h, k), index(y, z - ALONG_Z[1], hh)) for hh in range(2)]
    a1_sources = [(samp(ll, k), index(y, z + ALONG_Z[1], l)) for ll in range(2)]
    y_across = {e: (samp(1 - l, e // SIDE), index(y - e, z, h)) for e in (0, 1, 7)}
    y_across_sources = [(samp(1 - l, kk), index(y + 7 * k, z, h)) for kk in range(2)]
    y_across_core_0 = [(samp(1 - l, kk), index(y + 1, z, h)) for kk in range(2)]
    y_offsets = (0, 1, 7, 2, 6, 3, 5)
    y_targets = {e: (samp(l, e // SIDE), index(y - e, z, h)) for e in y_offsets}
    y_onward = (samp(l, 1), index(y - 2 + 4 * k, z, h))
    z_onward = z_targets[0]
    y_sources = [
        (samp(l, kk), index(y + (4 * k + b if b else k * (2 - 4 * kk)), z, h))
        for b in range(SIDE)
        for kk in range(2)
    ]
    beside = (samp(1 - l, k), block)
    sibling = (samp(l, 1 - k), block)
    ax_targets = [(samp(h, k), index(y, z, hh)) for hh in range(2)]
    ax_sources = [(samp(ll, k), index(y, z, l)) for ll in range(2)]
    a4_across = [(samp(h, 1 - k), index(y, z, hh)) for hh in range(2)]
    a4_across_sources = [(samp(ll, 1 - k), index(y, z, l)) for ll in range(2)]

    owners = []
    for slot in range(SIDE):
        offset = jnp.where(shift == 0, ALONG_Z[slot], ALONG_Z[slot + 1])
        owners.append((index(y, z + offset, l), h * 8 + k * 4 + slot))
    for slot in range(SIDE):
        owners.append((index(y + 4 * k + slot, z, h), 16 + l * 8 + k * 4 + slot))

    barrier = pltpu.get_barrier_semaphore()
    for source in peers + z_sources + y_sources[1:] + [beside, sibling] + a4_across_sources + (
        a1_sources + y_across_sources
    ):
        pl.semaphore_signal(barrier, inc=1, device_id=source, device_id_type=MESH)
    for source in y_across_core_0:
        pl.when(k == 0)(
            lambda source=source: pl.semaphore_signal(
                barrier, inc=1, device_id=source, device_id_type=MESH
            )
        )
    for source in [y_sources[0]] + ax_sources:
        unless_me(
            source,
            lambda source=source: pl.semaphore_signal(
                barrier, inc=1, device_id=source, device_id_type=MESH
            ),
        )
    for copy in own:
        copy.wait()
    pl.semaphore_wait(barrier, 24 - (1 - k) - same)

    sent = []
    small = []
    for n, peer in enumerate(peers):
        copy = send(own_part, own_part, small_send.at[n], small_recv.at[2 - n], peer)
        copy.start()
        small.append(copy)

    def send_y(e):
        slot = e % SIDE
        deliver = send_or_copy if e == 0 else send_on
        dst = bbuf.at[slot, k, l]
        sent.append(deliver(unit, dst, y_send.at[e], y_recv.at[slot], y_targets[e]))
        if e in y_across:
            sem = y_send.at[8 + e]
            sent.append(send_on(unit, dst, sem, bx_recv.at[slot], y_across[e]))

    def send_z(n):
        sem = z_send.at[n]
        sent.append(send_on(unit, line.at[n], sem, z_recv.at[n], z_targets[n - 1]))

    def send_slot(slot, targets):
        for n, target in enumerate(targets):
            deliver = send_or_copy if slot == 0 else send_on
            dst, sem = abuf.at[slot, k, l], ax_send.at[slot, n]
            sent.append(deliver(unit, dst, sem, ax_recv.at[slot], target))

    send_y(1)
    send_y(7)
    send_slot(1, a1_targets)
    send_slot(0, ax_targets)
    send_z(1)
    send_y(2)
    send_y(6)
    send_y(0)
    send_z(2)
    send_y(3)
    send_y(5)

    def pass_a(slot):
        src = line.at[slot - 1]
        landing(src, z_recv.at[slot - 1])
        for n, target in enumerate(ax_targets):
            dst = abuf.at[slot, k, l]
            sent.append(send_or_copy(src, dst, ax_send.at[slot, n], ax_recv.at[slot], target))
            if slot == 4:
                sem, sem_there = ax_send.at[slot, 2 + n], core_recv.at[slot]
                sent.append(send_on(src, dst, sem, sem_there, a4_across[n]))
        if slot == 2:
            copy = send(src, line.at[3], z_send.at[3], z_recv.at[3], z_onward)
            copy.start()
            sent.append(copy.wait_send)

    b_order = (1 + 2 * k, 2, k, 3 - 3 * k)

    def pass_b(step):
        slot = b_order[step]
        half = bbuf.at[slot, :, l]
        landing(half, y_recv.at[slot])
        if step == 0:
            return
        copy = send(half, half, bx_send.at[step], bx_recv.at[slot], beside)
        if step == 2:
            pl.when(k == 1)(copy.start)
            sent.append(lambda: pl.when(k == 1)(copy.wait_send))
        else:
            copy.start()
            sent.append(copy.wait_send)
        if step == 1:
            copy = send(bbuf.at[2, k, l], bbuf.at[0, k, l], y_send.at[4], y_recv.at[0], y_onward)
            copy.start()
            sent.append(copy.wait_send)

    def pass_core(slot):
        part = abuf.at[slot, k]
        landing(part, ax_recv.at[slot])
        copy = send(part, part, core_send.at[slot], core_recv.at[slot], sibling)
        copy.start()
        sent.append(copy.wait_send)

    for copy in small:
        copy.wait()
    both = jnp.concatenate([covb[n] for n in range(4)], axis=1)
    cov_t, trait_t = both[: cov.shape[0]], both[cov.shape[0] :]
    width, count = cov_t.shape
    eye = (
        lax.broadcasted_iota(jnp.int32, (width, width), 0)
        == lax.broadcasted_iota(jnp.int32, (width, width), 1)
    ).astype(jnp.float32)
    swept = dot(cov_t, cov_t, ((1,), (1,)), HIGHEST) + count / 10.0 * eye
    pass_a(2)
    pass_b(1)
    swept = sweep(swept, 0, 20)
    pass_core(0)
    pass_b(2)
    pass_a(3)
    pass_core(1)
    swept = sweep(swept, 20, width)
    pass_core(2)
    pass_b(0)
    pass_a(4)
    pass_b(3)
    solved = dot(-swept, cov_t, precision=HIGHEST)
    hat = dot(cov_t, solved, ((0,), (0,)), HIGHEST)
    diagonal = lax.broadcasted_iota(jnp.int32, (count, count), 0) == lax.broadcasted_iota(
        jnp.int32, (count, count), 1
    )
    project = jnp.where(diagonal, 1.0, 0.0) - hat
    high, low = split(project)
    pcat[:, :count] = high
    pcat[:, count:] = low
    scaled = dot(trait_t, project, precision=HIGHEST) * (1.0 / math.sqrt(count))
    ysc[...] = scaled
    traits_id = lax.broadcasted_iota(jnp.int32, (scaled.shape[0], 1), 0)
    tw_col = sum(jnp.where(traits_id == t, tw[t], 0.0) for t in range(scaled.shape[0]))
    qmat[...] = dot(scaled * tw_col, scaled, ((0,), (0,)), HIGHEST)
    pass_core(3)
    def prepare(genotypes, ats, rcat, rfull, hrows):
        genotypes = [g.astype(jnp.float32).reshape(count, 128) for g in genotypes]
        centred = (jnp.concatenate(genotypes, axis=1) - 1.0).astype(jnp.bfloat16)
        resids = dot(pcat[...], jnp.concatenate([centred, centred], axis=0))
        for n, (at, hrow) in enumerate(zip(ats, hrows)):
            resid = resids[:, n * 128 : (n + 1) * 128]
            high, low = split(resid)
            at = pl.ds(pl.multiple_of(at * 128, 128), 128)
            rfull[:, at] = 2.0 * resid - high.astype(jnp.float32)
            rcat[:count, at] = high
            rcat[count:, at] = high
            gram = dot(
                jnp.concatenate([high, low + low], axis=1),
                jnp.concatenate([high, high], axis=1),
                ((1,), (1,)),
            )
            h_high, h_low = split(gram * qmat[...])
            rows = pl.ds(pl.multiple_of(hrow * count, count), count)
            hcat[rows, :count] = h_high
            hcat[rows, count:] = h_low

    def prepare_b(first):
        slots = [first, first + 1]
        for slot in slots:
            landing(bbuf.at[slot, :, 1 - l], bx_recv.at[slot])
        hrows = [A_SLOTS + slot for slot in slots]
        prepare([bbuf[slot] for slot in slots], slots, rcat_b, rfull_b, hrows)

    def prepare_a(*slots):
        for slot in slots:
            if slot == 4:
                landing(abuf.at[slot, k], ax_recv.at[slot])
            landing(abuf.at[slot, 1 - k], core_recv.at[slot])
        prepare([abuf[slot] for slot in slots], slots, rcat_a, rfull_a, slots)

    def pairs(hrow, number, rcat, rfull, at):
        at = pl.ds(pl.multiple_of(at * 128, 128), 256)
        rows = pl.ds(pl.multiple_of(hrow * count, count), number * count)
        product = dot(hcat[rows, :], rcat[:, at])
        weighted = product.reshape(number, count, 256) * rfull[:, at][None]
        sums = jnp.sum(weighted, axis=1)
        return jnp.concatenate([sums, jnp.zeros((8 - number, 256), jnp.float32)], axis=0)

    row_ids = lax.broadcasted_iota(jnp.int32, (8, 128), 0)

    def give_back(slot):
        owner, at = owners[slot]
        for q in range(4):
            sem = out_send.at[slot * 4 + q]
            deliver = send_or_copy if slot in (0, SIDE) else send_on
            kind = out_recv.at[slot // SIDE]
            sent.append(deliver(tiles.at[slot], landed.at[at], sem, kind, (q, owner)))

    near, rest = 2 * k, 2 - 2 * k

    def add(at, part, fresh):
        tiles[at] = part if fresh else tiles[at] + part

    def score_a(part, number, first, fresh):
        sums = pairs(A_SLOTS + first, number, rcat_a, rfull_a, shift + 2 * part)
        sums = pltpu.roll(sums, 4 * k + first, 0)
        add(2 * part, sums[:, :128], fresh)
        add(2 * part + 1, sums[:, 128:], fresh)

    def score_b(first, of_a, number, fresh):
        sums = pairs(shift + 2 * of_a, number, rcat_b, rfull_b, first)
        sums = pltpu.roll(sums, shift + 2 * of_a, 0)
        picked = [sums[a : a + 1] for a in (0, 5, 6, 3, 4, 7, 2, 1)]
        sums = jnp.concatenate(picked, axis=0)
        add(SIDE + first, sums[:, :128], fresh)
        add(SIDE + first + 1, sums[:, 128:], fresh)

    prepare_b(near)
    prepare_a(0, 1)
    prepare_a(2)
    score_a(0, 2, near, True)
    score_b(near, 0, 2, True)
    prepare_b(rest)
    score_a(0, 2, rest, False)
    score_b(rest, 0, 2, True)

    @pl.when((same == 1) & (k == 0))
    def _():
        resid = 0.5 * (rfull_a[:, :128] + rcat_a[:count, :128].astype(jnp.float32))
        diag = dot(ysc[...], resid * resid, precision=HIGHEST)
        diag = jnp.sum(diag * diag * tw_col, axis=0, keepdims=True)
        tiles[0] = tiles[0] - jnp.where(row_ids == 0, diag, 0.0)

    give_back(1)
    give_back(0)
    prepare_a(3, 4)
    score_a(1, 4, 0, True)
    give_back(3)
    give_back(2)
    score_b(2, 1, 2, False)
    give_back(7)
    give_back(6)
    score_b(0, 1, 2, False)

    @pl.when(same == 1)
    def _():
        rows = pl.ds(pl.multiple_of((1 - k) * 4 * count, count), count)
        product = dot(hcat[rows, :], rcat_b[:, :128])
        extra = jnp.sum(product * rfull_b[:, :128], axis=0, keepdims=True)
        tile = jnp.where(row_ids == 4 * k, 0.0, tiles[SIDE])
        tiles[SIDE] = jnp.where(row_ids == 4 * (1 - k), extra, tile)

    give_back(4)
    give_back(5)

    sum_a[...] = jnp.zeros_like(sum_a)
    for wait in sent:
        wait()
    landing(landed.at[:16], out_recv.at[0])
    for i in range(2):
        mixed = jnp.not_equal(h, i).astype(jnp.int32)
        for kk in range(2):
            first = mixed * (1 - h) + (1 - mixed) * kk
            for n in range(SIDE):
                offset = jnp.where(first == 0, ALONG_Z[n], ALONG_Z[n + 1])
                there = pl.ds((z + 8 - offset) % 8 * 2 + i, 8, stride=16)
                sum_a[there, :] = sum_a[there, :] + pltpu.roll(landed[i * 8 + kk * 4 + n], y, 0)
    landing(landed.at[16:], out_recv.at[1])
    for i in range(2):
        for e in range(8):
            there = pl.ds((y + 8 - e) % 8 * 16 + i, 8, stride=2)
            sum_b[there, :] = pltpu.roll(landed[16 + i * 8 + e], z, 0)
    out[...] = (sum_a[...] + sum_b[...]).T * (1.0 / out.shape[0])


def body(genotypes, covariates, traits, trait_weights):
    part, width = genotypes.shape
    count = 4 * part
    cov_count, trait_count = covariates.shape[1], traits.shape[1]
    f32, bf16, i32 = jnp.float32, jnp.bfloat16, jnp.int32
    dma = pltpu.SemaphoreType.DMA
    inputs = (genotypes, covariates.T, traits.T, trait_weights)
    held = [pltpu.with_memory_space_constraint(value, pltpu.HBM) for value in inputs]
    return pl.pallas_call(
        kernel,
        name="epistasis",
        out_shape=jax.ShapeDtypeStruct((width, 128), f32),
        in_specs=[pl.BlockSpec(memory_space=pl.ANY)] * 4,
        out_specs=pl.BlockSpec(memory_space=pltpu.VMEM),
        scratch_shapes=[
            pltpu.VMEM((part, width), i32),
            pltpu.VMEM((A_SLOTS - 1, part, width), i32),
            pltpu.VMEM((A_SLOTS, 2, 2, part, width), i32),
            pltpu.VMEM((SIDE, 2, 2, part, width), i32),
            pltpu.VMEM((4, cov_count + trait_count, part), f32),
            pltpu.SMEM((trait_count,), f32),
            pltpu.VMEM((count, 2 * count), bf16),
            pltpu.VMEM((count, count), f32),
            pltpu.VMEM((trait_count, count), f32),
            pltpu.VMEM(((A_SLOTS + SIDE) * count, 2 * count), bf16),
            pltpu.VMEM((2 * count, A_SLOTS * width), bf16),
            pltpu.VMEM((2 * count, SIDE * width), bf16),
            pltpu.VMEM((count, A_SLOTS * width), f32),
            pltpu.VMEM((count, SIDE * width), f32),
            pltpu.VMEM((2 * SIDE, 8, width), f32),
            pltpu.VMEM((32, 8, width), f32),
            pltpu.VMEM((128, width), f32),
            pltpu.VMEM((128, width), f32),
            dma((4,)), dma((4,)), dma((16,)), dma((SIDE,)), dma((SIDE,)), dma((SIDE,)),
            dma((A_SLOTS, 4)), dma((A_SLOTS,)), dma((A_SLOTS,)), dma((A_SLOTS,)),
            dma((3,)), dma((3,)), dma((4,)), dma((32,)), dma((2,)),
        ],
        compiler_params=pltpu.CompilerParams(
            collective_id=0, has_side_effects=True, vmem_limit_bytes=32 << 20
        ),
    )(*held)


def solution(mesh):
    placed = (P("samp", "var"), P("samp", None), P("samp", None), P())
    return jax.shard_map(
        body, mesh=mesh, in_specs=placed, out_specs=P("var", None), check_vma=False
    )
```

```python
import math

import jax
import jax.numpy as jnp
from jax import lax
from jax.experimental import pallas as pl
from jax.experimental.pallas import tpu as pltpu
from jax.sharding import PartitionSpec as P

MESH = pl.DeviceIdType.MESH
HIGHEST = lax.Precision.HIGHEST
SIDE = 4
ALONG_Z = (0, -1, -2, 3, 4)
A_SLOTS = len(ALONG_Z)


def dot(a, b, contract=((1,), (0,)), precision=None):
    return lax.dot_general(
        a, b, (contract, ((), ())), precision=precision, preferred_element_type=jnp.float32
    )


def split(value):
    high = value.astype(jnp.bfloat16)
    return high, (value - high.astype(jnp.float32)).astype(jnp.bfloat16)


def sweep(matrix, begin, end):
    size = matrix.shape[0]
    rows = lax.broadcasted_iota(jnp.int32, (size, size), 0)
    cols = lax.broadcasted_iota(jnp.int32, (size, size), 1)
    for k in range(begin, end, 2):
        row_1, row_2 = matrix[k : k + 1, :], matrix[k + 1 : k + 2, :]
        col_1 = jnp.broadcast_to(matrix[:, k : k + 1], (size, size))
        col_2 = jnp.broadcast_to(matrix[:, k + 1 : k + 2], (size, size))
        p, q, r = col_1[k : k + 1, :], col_2[k : k + 1, :], col_2[k + 1 : k + 2, :]
        scale = 1.0 / (p * r - q * q)
        row_1 = jnp.where(cols[:1] == k, -1.0, jnp.where(cols[:1] == k + 1, 0.0, row_1))
        row_2 = jnp.where(cols[:1] == k + 1, -1.0, jnp.where(cols[:1] == k, 0.0, row_2))
        col_1 = jnp.where(rows == k, -1.0, jnp.where(rows == k + 1, 0.0, col_1))
        col_2 = jnp.where(rows == k + 1, -1.0, jnp.where(rows == k, 0.0, col_2))
        kept = (rows == k) | (rows == k + 1) | (cols == k) | (cols == k + 1)
        matrix = (
            jnp.where(kept, 0.0, matrix)
            - col_1 * ((r * row_1 - q * row_2) * scale)
            - col_2 * ((p * row_2 - q * row_1) * scale)
        )
    return matrix


def kernel(
    geno, cov, trait, weights, out,
    unit, line, abuf, bbuf, covb, tw, pcat, qmat, ysc, hcat, rcat_a, rcat_b, rfull_a, rfull_b,
    tiles, landed, sum_a, sum_b,
    z_send, z_recv, y_send, y_recv, bx_send, bx_recv, ax_send, ax_recv, core_send, core_recv,
    small_send, small_recv, own_sem, out_send, out_recv,
):
    section = lax.axis_index("samp")
    block = lax.axis_index("var")
    l, k = section // 2, section % 2
    h, z, y = block % 2, (block // 2) % 8, block // 16
    same = (h == l).astype(jnp.int32)
    shift = same * k + (1 - same) * h

    def index(yy, zz, hh):
        return (lax.rem(yy + 16, 8) * 8 + lax.rem(zz + 16, 8)) * 2 + hh

    def samp(ll, kk):
        return 2 * ll + kk

    def is_me(target):
        return (target[0] == section) & (target[1] == block)

    def unless_me(target, action):
        pl.when(jnp.logical_not(is_me(target)))(action)

    def send(src, dst, send_sem, recv_sem, target):
        return pltpu.make_async_remote_copy(
            src_ref=src, dst_ref=dst, send_sem=send_sem, recv_sem=recv_sem,
            device_id=target, device_id_type=MESH,
        )

    def send_or_copy(src, dst, send_sem, recv_sem, target):
        mine = is_me(target)
        remote = send(src, dst, send_sem, recv_sem, target)
        pl.when(jnp.logical_not(mine))(remote.start)
        pl.when(mine)(pltpu.make_async_copy(src, dst, recv_sem).start)
        return lambda: unless_me(target, remote.wait_send)

    def send_on(src, dst, send_sem, recv_sem, target):
        remote = send(src, dst, send_sem, recv_sem, target)
        remote.start()
        return remote.wait_send

    def landing(ref, sem):
        pltpu.make_async_copy(ref, ref, sem).wait()

    own_part = covb.at[2 * k + l]
    own = [
        pltpu.make_async_copy(cov, own_part.at[: cov.shape[0]], own_sem.at[0]),
        pltpu.make_async_copy(trait, own_part.at[cov.shape[0] :], own_sem.at[1]),
        pltpu.make_async_copy(weights, tw, own_sem.at[2]),
        pltpu.make_async_copy(geno, unit, own_sem.at[3]),
    ]
    for copy in own:
        copy.start()

    peers = [((section + step) % 4, block) for step in range(1, 4)]
    z_targets = [(section, index(y, z - d, h)) for d in ALONG_Z[2:4]]
    z_sources = [(section, index(y, z + d, h)) for d in ALONG_Z[2:4]]
    a1_targets = [(samp(h, k), index(y, z - ALONG_Z[1], hh)) for hh in range(2)]
    a1_sources = [(samp(ll, k), index(y, z + ALONG_Z[1], l)) for ll in range(2)]
    y_across = {e: (samp(1 - l, e // SIDE), index(y - e, z, h)) for e in (0, 1, 7)}
    y_across_sources = [(samp(1 - l, kk), index(y + 7 * k, z, h)) for kk in range(2)]
    y_across_core_0 = [(samp(1 - l, kk), index(y + 1, z, h)) for kk in range(2)]
    y_offsets = (0, 1, 7, 2, 6, 3, 5)
    y_targets = {e: (samp(l, e // SIDE), index(y - e, z, h)) for e in y_offsets}
    y_onward = (samp(l, 1), index(y - 2 + 4 * k, z, h))
    z_onward = z_targets[0]
    y_sources = [
        (samp(l, kk), index(y + (4 * k + b if b else k * (2 - 4 * kk)), z, h))
        for b in range(SIDE)
        for kk in range(2)
    ]
    beside = (samp(1 - l, k), block)
    sibling = (samp(l, 1 - k), block)
    ax_targets = [(samp(h, k), index(y, z, hh)) for hh in range(2)]
    ax_sources = [(samp(ll, k), index(y, z, l)) for ll in range(2)]
    a4_across = [(samp(h, 1 - k), index(y, z, hh)) for hh in range(2)]
    a4_across_sources = [(samp(ll, 1 - k), index(y, z, l)) for ll in range(2)]

    owners = []
    for slot in range(SIDE):
        offset = jnp.where(shift == 0, ALONG_Z[slot], ALONG_Z[slot + 1])
        owners.append((index(y, z + offset, l), h * 8 + k * 4 + slot))
    for slot in range(SIDE):
        owners.append((index(y + 4 * k + slot, z, h), 16 + l * 8 + k * 4 + slot))

    barrier = pltpu.get_barrier_semaphore()
    for source in peers + z_sources + y_sources[1:] + [beside, sibling] + a4_across_sources + (
        a1_sources + y_across_sources
    ):
        pl.semaphore_signal(barrier, inc=1, device_id=source, device_id_type=MESH)
    for source in y_across_core_0:
        pl.when(k == 0)(
            lambda source=source: pl.semaphore_signal(
                barrier, inc=1, device_id=source, device_id_type=MESH
            )
        )
    for source in [y_sources[0]] + ax_sources:
        unless_me(
            source,
            lambda source=source: pl.semaphore_signal(
                barrier, inc=1, device_id=source, device_id_type=MESH
            ),
        )
    for copy in own:
        copy.wait()
    pl.semaphore_wait(barrier, 24 - (1 - k) - same)

    sent = []
    small = []
    for n, peer in enumerate(peers):
        copy = send(own_part, own_part, small_send.at[n], small_recv.at[2 - n], peer)
        copy.start()
        small.append(copy)

    def send_y(e):
        slot = e % SIDE
        deliver = send_or_copy if e == 0 else send_on
        dst = bbuf.at[slot, k, l]
        sent.append(deliver(unit, dst, y_send.at[e], y_recv.at[slot], y_targets[e]))
        if e in y_across:
            sem = y_send.at[8 + e]
            sent.append(send_on(unit, dst, sem, bx_recv.at[slot], y_across[e]))

    def send_z(n):
        sem = z_send.at[n]
        sent.append(send_on(unit, line.at[n], sem, z_recv.at[n], z_targets[n - 1]))

    def send_slot(slot, targets):
        for n, target in enumerate(targets):
            deliver = send_or_copy if slot == 0 else send_on
            dst, sem = abuf.at[slot, k, l], ax_send.at[slot, n]
            sent.append(deliver(unit, dst, sem, ax_recv.at[slot], target))

    send_y(1)
    send_y(7)
    send_slot(1, a1_targets)
    send_slot(0, ax_targets)
    send_z(1)
    send_y(2)
    send_y(6)
    send_y(0)
    send_z(2)
    send_y(3)
    send_y(5)

    def pass_a(slot):
        src = line.at[slot - 1]
        landing(src, z_recv.at[slot - 1])
        for n, target in enumerate(ax_targets):
            dst = abuf.at[slot, k, l]
            sent.append(send_or_copy(src, dst, ax_send.at[slot, n], ax_recv.at[slot], target))
            if slot == 4:
                sem, sem_there = ax_send.at[slot, 2 + n], core_recv.at[slot]
                sent.append(send_on(src, dst, sem, sem_there, a4_across[n]))
        if slot == 2:
            copy = send(src, line.at[3], z_send.at[3], z_recv.at[3], z_onward)
            copy.start()
            sent.append(copy.wait_send)

    b_order = (1 + 2 * k, 2, k, 3 - 3 * k)

    def pass_b(step):
        slot = b_order[step]
        half = bbuf.at[slot, :, l]
        landing(half, y_recv.at[slot])
        if step == 0:
            return
        copy = send(half, half, bx_send.at[step], bx_recv.at[slot], beside)
        if step == 2:
            pl.when(k == 1)(copy.start)
            sent.append(lambda: pl.when(k == 1)(copy.wait_send))
        else:
            copy.start()
            sent.append(copy.wait_send)
        if step == 1:
            copy = send(bbuf.at[2, k, l], bbuf.at[0, k, l], y_send.at[4], y_recv.at[0], y_onward)
            copy.start()
            sent.append(copy.wait_send)

    def pass_core(slot):
        part = abuf.at[slot, k]
        landing(part, ax_recv.at[slot])
        copy = send(part, part, core_send.at[slot], core_recv.at[slot], sibling)
        copy.start()
        sent.append(copy.wait_send)

    for copy in small:
        copy.wait()
    both = jnp.concatenate([covb[n] for n in range(4)], axis=1)
    cov_t, trait_t = both[: cov.shape[0]], both[cov.shape[0] :]
    width, count = cov_t.shape
    eye = (
        lax.broadcasted_iota(jnp.int32, (width, width), 0)
        == lax.broadcasted_iota(jnp.int32, (width, width), 1)
    ).astype(jnp.float32)
    swept = dot(cov_t, cov_t, ((1,), (1,)), HIGHEST) + count / 10.0 * eye
    pass_a(2)
    pass_b(1)
    swept = sweep(swept, 0, 20)
    pass_core(0)
    pass_b(2)
    pass_a(3)
    pass_core(1)
    swept = sweep(swept, 20, width)
    pass_core(2)
    pass_b(0)
    pass_a(4)
    pass_b(3)
    solved = dot(-swept, cov_t, precision=HIGHEST)
    hat = dot(cov_t, solved, ((0,), (0,)), HIGHEST)
    diagonal = lax.broadcasted_iota(jnp.int32, (count, count), 0) == lax.broadcasted_iota(
        jnp.int32, (count, count), 1
    )
    project = jnp.where(diagonal, 1.0, 0.0) - hat
    high, low = split(project)
    pcat[:, :count] = high
    pcat[:, count:] = low
    scaled = dot(trait_t, project, precision=HIGHEST) * (1.0 / math.sqrt(count))
    ysc[...] = scaled
    traits_id = lax.broadcasted_iota(jnp.int32, (scaled.shape[0], 1), 0)
    tw_col = sum(jnp.where(traits_id == t, tw[t], 0.0) for t in range(scaled.shape[0]))
    qmat[...] = dot(scaled * tw_col, scaled, ((0,), (0,)), HIGHEST)
    pass_core(3)
    def prepare(genotypes, ats, rcat, rfull, hrows):
        genotypes = [g.astype(jnp.float32).reshape(count, 128) for g in genotypes]
        centred = (jnp.concatenate(genotypes, axis=1) - 1.0).astype(jnp.bfloat16)
        resids = dot(pcat[...], jnp.concatenate([centred, centred], axis=0))
        for n, (at, hrow) in enumerate(zip(ats, hrows)):
            resid = resids[:, n * 128 : (n + 1) * 128]
            high, low = split(resid)
            at = pl.ds(pl.multiple_of(at * 128, 128), 128)
            rfull[:, at] = 2.0 * resid - high.astype(jnp.float32)
            rcat[:count, at] = high
            rcat[count:, at] = high
            gram = dot(
                jnp.concatenate([high, low + low], axis=1),
                jnp.concatenate([high, high], axis=1),
                ((1,), (1,)),
            )
            h_high, h_low = split(gram * qmat[...])
            rows = pl.ds(pl.multiple_of(hrow * count, count), count)
            hcat[rows, :count] = h_high
            hcat[rows, count:] = h_low

    def prepare_b(first):
        slots = [first, first + 1]
        for slot in slots:
            landing(bbuf.at[slot, :, 1 - l], bx_recv.at[slot])
        hrows = [A_SLOTS + slot for slot in slots]
        prepare([bbuf[slot] for slot in slots], slots, rcat_b, rfull_b, hrows)

    def prepare_a(*slots):
        for slot in slots:
            if slot == 4:
                landing(abuf.at[slot, k], ax_recv.at[slot])
            landing(abuf.at[slot, 1 - k], core_recv.at[slot])
        prepare([abuf[slot] for slot in slots], slots, rcat_a, rfull_a, slots)

    def pairs(hrow, number, rcat, rfull, at):
        at = pl.ds(pl.multiple_of(at * 128, 128), 256)
        rows = pl.ds(pl.multiple_of(hrow * count, count), number * count)
        product = dot(hcat[rows, :], rcat[:, at])
        weighted = product.reshape(number, count, 256) * rfull[:, at][None]
        sums = jnp.sum(weighted, axis=1)
        return jnp.concatenate([sums, jnp.zeros((8 - number, 256), jnp.float32)], axis=0)

    row_ids = lax.broadcasted_iota(jnp.int32, (8, 128), 0)

    def give_back(slot):
        owner, at = owners[slot]
        for q in range(4):
            sem = out_send.at[slot * 4 + q]
            deliver = send_or_copy if slot in (0, SIDE) else send_on
            kind = out_recv.at[slot // SIDE]
            sent.append(deliver(tiles.at[slot], landed.at[at], sem, kind, (q, owner)))

    near, rest = 2 * k, 2 - 2 * k

    def add(at, part, fresh):
        tiles[at] = part if fresh else tiles[at] + part

    def score_a(part, number, first, fresh):
        sums = pairs(A_SLOTS + first, number, rcat_a, rfull_a, shift + 2 * part)
        sums = pltpu.roll(sums, 4 * k + first, 0)
        add(2 * part, sums[:, :128], fresh)
        add(2 * part + 1, sums[:, 128:], fresh)

    def score_b(first, of_a, number, fresh):
        sums = pairs(shift + 2 * of_a, number, rcat_b, rfull_b, first)
        sums = pltpu.roll(sums, shift + 2 * of_a, 0)
        picked = [sums[a : a + 1] for a in (0, 5, 6, 3, 4, 7, 2, 1)]
        sums = jnp.concatenate(picked, axis=0)
        add(SIDE + first, sums[:, :128], fresh)
        add(SIDE + first + 1, sums[:, 128:], fresh)

    prepare_b(near)
    prepare_a(0, 1)
    prepare_a(2)
    score_a(0, 2, near, True)
    score_b(near, 0, 2, True)
    prepare_b(rest)
    score_a(0, 2, rest, False)
    score_b(rest, 0, 2, True)

    @pl.when((same == 1) & (k == 0))
    def _():
        resid = 0.5 * (rfull_a[:, :128] + rcat_a[:count, :128].astype(jnp.float32))
        diag = dot(ysc[...], resid * resid, precision=HIGHEST)
        diag = jnp.sum(diag * diag * tw_col, axis=0, keepdims=True)
        tiles[0] = tiles[0] - jnp.where(row_ids == 0, diag, 0.0)

    give_back(1)
    give_back(0)
    prepare_a(3, 4)
    score_a(1, 4, 0, True)
    give_back(3)
    give_back(2)
    score_b(2, 1, 2, False)
    give_back(7)
    give_back(6)
    score_b(0, 1, 2, False)

    @pl.when(same == 1)
    def _():
        rows = pl.ds(pl.multiple_of((1 - k) * 4 * count, count), count)
        product = dot(hcat[rows, :], rcat_b[:, :128])
        extra = jnp.sum(product * rfull_b[:, :128], axis=0, keepdims=True)
        tile = jnp.where(row_ids == 4 * k, 0.0, tiles[SIDE])
        tiles[SIDE] = jnp.where(row_ids == 4 * (1 - k), extra, tile)

    give_back(4)
    give_back(5)

    sum_a[:128, :] = jnp.zeros((128, 128), jnp.float32)
    for wait in sent:
        wait()
    landing(landed.at[:16], out_recv.at[0])
    for i in range(2):
        mixed = jnp.not_equal(h, i).astype(jnp.int32)
        for kk in range(2):
            first = mixed * (1 - h) + (1 - mixed) * kk
            for n in range(SIDE):
                offset = jnp.where(first == 0, ALONG_Z[n], ALONG_Z[n + 1])
                there = pl.ds((z + 8 - offset) % 8 * 2 + i, 8, stride=16)
                sum_a[there, :] = sum_a[there, :] + pltpu.roll(landed[i * 8 + kk * 4 + n], y, 0)
    landing(landed.at[16:], out_recv.at[1])
    for i in range(2):
        for e in range(8):
            there = pl.ds((y + 8 - e) % 8 * 16 + i, 8, stride=2)
            sum_b[there, :] = pltpu.roll(landed[16 + i * 8 + e], z, 0)
    out[...] = (sum_a[:128, :] + sum_b[:128, :]).T * (1.0 / out.shape[0])


def body(genotypes, covariates, traits, trait_weights):
    part, width = genotypes.shape
    count = 4 * part
    cov_count, trait_count = covariates.shape[1], traits.shape[1]
    f32, bf16, i32 = jnp.float32, jnp.bfloat16, jnp.int32
    dma = pltpu.SemaphoreType.DMA
    inputs = (genotypes, covariates.T, traits.T, trait_weights)
    held = [pltpu.with_memory_space_constraint(value, pltpu.HBM) for value in inputs]
    return pl.pallas_call(
        kernel,
        name="epistasis",
        out_shape=jax.ShapeDtypeStruct((width, 128), f32),
        in_specs=[pl.BlockSpec(memory_space=pl.ANY)] * 4,
        out_specs=pl.BlockSpec(memory_space=pltpu.VMEM),
        scratch_shapes=[
            pltpu.VMEM((part, width), i32),
            pltpu.VMEM((A_SLOTS - 1, part, width), i32),
            pltpu.VMEM((A_SLOTS, 2, 2, part, width), i32),
            pltpu.VMEM((SIDE, 2, 2, part, width), i32),
            pltpu.VMEM((4, cov_count + trait_count, part), f32),
            pltpu.SMEM((trait_count,), f32),
            pltpu.VMEM((count, 2 * count), bf16),
            pltpu.VMEM((count, count), f32),
            pltpu.VMEM((trait_count, count), f32),
            pltpu.VMEM(((A_SLOTS + SIDE) * count, 2 * count), bf16),
            pltpu.VMEM((2 * count, A_SLOTS * width), bf16),
            pltpu.VMEM((2 * count, SIDE * width), bf16),
            pltpu.VMEM((count, A_SLOTS * width), f32),
            pltpu.VMEM((count, SIDE * width), f32),
            pltpu.VMEM((2 * SIDE, 8, width), f32),
            pltpu.VMEM((32, 8, width), f32),
            pltpu.VMEM((256, width), f32),
            pltpu.VMEM((256, width), f32),
            dma((4,)), dma((4,)), dma((16,)), dma((SIDE,)), dma((SIDE,)), dma((SIDE,)),
            dma((A_SLOTS, 4)), dma((A_SLOTS,)), dma((A_SLOTS,)), dma((A_SLOTS,)),
            dma((3,)), dma((3,)), dma((4,)), dma((32,)), dma((2,)),
        ],
        compiler_params=pltpu.CompilerParams(
            collective_id=0, has_side_effects=True, vmem_limit_bytes=32 << 20
        ),
    )(*held)


def solution(mesh):
    placed = (P("samp", "var"), P("samp", None), P("samp", None), P())
    return jax.shard_map(
        body, mesh=mesh, in_specs=placed, out_specs=P("var", None), check_vma=False
    )
```
